32 devices in a mesh: parts: 2 (over x), wide: 8 (over z, y), narrow: 2 (over core).
Axes of the slice: x: 2, y: 2, z: 4, core: 2. Of those that a mesh axis runs over, the one named last changes fastest.
Arguments:
- embeddings: bfloat16 [24576, 1024], P(('parts', 'wide', 'narrow')), parts along dimension 0, may hold values from -6 to 6
- labels: int32 [24576, 1], P(('parts', 'wide', 'narrow')), parts along dimension 0, may hold values from 0 to 7; in each aligned block of 768 rows (0 to 767, 768 to 1535, ...) at most 192 rows name the same one
- priority: int32 [24576], P(('parts', 'wide', 'narrow')), parts along dimension 0, may hold values from 0 to 12287, each once
Outputs:
- best_match: float32 [24576], P(('parts', 'wide', 'narrow')), parts along dimension 0
The draws below stay inside these ranges and needn't reach their ends.
There are 2 independent parts, one for each index of `parts`. The reference program is written for one: setup_inputs(seed, part) draws one part's arguments, and reference() takes and returns one part's arrays. A program takes and returns all parts, laid end to end along the dimension named above; each array names one. Nothing has to cross between parts.
Inputs may be any that keep to these rules, and one draw needn't show every extreme that they name: `labels`: among the rows of one device at most 192 carry one label; in every draw some device has 192 rows of one label. `priority`: all priorities are distinct.
All inputs are finite; a program needn't handle non-finite values.
Results may differ from the reference program's by a relative error of at most 0.0014.
Values may be sent and summed in bfloat16 or wider, within the bound.
No kernel may reach another device: no remote copies, remote signals or barrier semaphores. Data moves between devices by JAX's collectives and lax.ppermute only.
A program may use at most 64 MiB of HBM per device.

```python
import math
import jax
import jax.numpy as jnp
import numpy as np
from jax import lax

D = 1024
ROWS_DEV = 768
CAP = 192
CLUSTERS = 8
ROWS = 12288
N_WIDE = 8
N_NARROW = 2


def levels(stream_key, shape, split, low, high):
    level = 1.0
    for position, parts in split:
        heights = jax.random.uniform(jax.random.fold_in(jax.random.fold_in(stream_key, 6), position), (parts,), jnp.float32, low / len(split), high / len(split))
        level = level * jnp.repeat(jnp.exp(heights), shape[position] // parts).reshape((-1,) + (1,) * (len(shape) - 1 - position))
    return level


def assign_block(own_key, own, number, rows, number_of, top, bound, lean):
    ranking = jax.random.permutation(own_key, number_of)
    crowded, usual = shares(number_of, rows * top, bound, lean, True), shares(number_of, rows * top, bound, lean, False)
    places = jnp.arange(number_of)

    def named(tallies, offset_by):
        used = int((tallies > 0).sum())
        fixed = max(1, used // 4)
        passed = fixed + (places - fixed + offset_by * (used - fixed)) % max(1, number_of - fixed)
        return jnp.zeros((number_of,), jnp.int32).at[ranking[jnp.where(places < fixed, places, passed)]].set(jnp.asarray(tallies, jnp.int32))

    tallies = jnp.where(number % 4 == 0, named(crowded, number // 4), named(usual, number - number // 4 - 1))
    mixed = jax.random.permutation(jax.random.fold_in(own, 3), number_of)
    source_of, sink = mixed[0:number_of // 2 * 2:2], mixed[1:number_of // 2 * 2:2]
    margin = jnp.minimum(tallies[source_of] - 1, bound - tallies[sink]) // 2
    margin = jnp.where((source_of == ranking[0]) | (sink == ranking[0]) | (tallies[sink] == 0), 0, jnp.maximum(margin, 0))
    passed = jax.random.randint(jax.random.fold_in(own, 4), (number_of // 2,), 0, 1 << 20) % (margin + 1)
    tallies = tallies.at[source_of].add(-passed).at[sink].add(passed)
    items = jnp.searchsorted(jnp.cumsum(tallies), jnp.arange(rows * top), side="right").astype(jnp.int32)
    listing = items.reshape(top, rows).T
    listing = listing[jax.random.permutation(jax.random.fold_in(own, 1), rows)]
    offset_by = jax.random.randint(jax.random.fold_in(own, 2), (rows, 1), 0, top)
    return jnp.take_along_axis(listing, (jnp.arange(top)[None, :] + offset_by) % top, axis=1)


def shares(number_of, total, bound, slope, full):
    loads = [(1 << 20) // math.isqrt(rank ** slope) + 1 for rank in range(1, number_of + 1)]
    largest = bound if full else min(bound, max(-(-total // number_of), total * loads[0] // sum(loads)))
    least = 1 if total - largest >= number_of - 1 else 0
    given, surplus = [largest] + [least] * (number_of - 1), total - largest - least * (number_of - 1)
    while surplus > 0:
        movable = [i for i in range(1, number_of) if given[i] < largest] or [i for i in range(1, number_of) if given[i] < bound]
        mass, budget = sum([loads[i] for i in movable]), surplus
        for i in movable:
            extra = min(bound - given[i], max(1, budget * loads[i] // mass), surplus)
            given[i] = given[i] + extra
            surplus = surplus - extra
    return np.array(given)


def scatter_about(own_key, dims, width, bound, shards=(), held_as=jnp.bfloat16):
    drawn = width * jax.random.normal(own_key, dims, jnp.float32)
    if shards:
        drawn = drawn * levels(own_key, dims, shards, -0.22, 0.18)
    return jnp.clip(drawn, -bound, bound).astype(held_as)


def setup_inputs(seed: int = 0, part: int = 0) -> dict:
    arg_keys = jax.random.split(jax.random.key(seed), 4)
    part_keys = jax.random.split(jax.random.fold_in(arg_keys[3], part), 4)
    embeddings = scatter_about(part_keys[0], (ROWS, D), 1.0, 6.0, ((0, 16),))
    labels_keys = jax.random.split(jax.random.fold_in(part_keys[1], 1), ROWS // ROWS_DEV)
    labels_turns = jax.random.permutation(jax.random.fold_in(part_keys[1], 3), ROWS // ROWS_DEV)
    labels = jax.vmap(lambda own, number: assign_block(jax.random.fold_in(part_keys[1], 2), own, number, ROWS_DEV, CLUSTERS, 1, CAP, 2))(labels_keys, labels_turns).reshape((ROWS, 1))
    priority = jax.random.permutation(part_keys[2], ROWS).astype(jnp.int32)
    return dict(embeddings=embeddings, labels=labels, priority=priority)


def reference(embeddings, labels, priority):
    emb = embeddings.astype(jnp.float32)
    unit = (emb * lax.rsqrt(lax.optimization_barrier(jnp.sum(emb * emb, axis=1, keepdims=True)) + 1e-06)).astype(jnp.bfloat16)
    lab = labels[:, 0]
    order = jnp.argsort(lab, stable=True).astype(jnp.int32)
    onehot = (lab[:, None] == jnp.arange(CLUSTERS, dtype=jnp.int32)[None, :]).astype(jnp.int32)
    counts = lax.optimization_barrier(jnp.sum(onehot, axis=0))
    starts = (jnp.cumsum(counts) - counts).astype(jnp.int32)
    most_rows = N_NARROW * N_WIDE * CAP
    order_pad = jnp.concatenate([order, jnp.zeros((most_rows,), jnp.int32)])
    total = ROWS

    def one_cluster(cluster):
        index = lax.dynamic_slice_in_dim(order_pad, starts[cluster], most_rows)
        valid = jnp.arange(most_rows, dtype=jnp.int32) < counts[cluster]
        rows = unit[index].astype(jnp.float32)
        ranks = jnp.where(valid, priority[index], -1)
        similar = jnp.dot(rows, rows.T, precision=lax.Precision.HIGHEST)
        mask = (ranks[None, :] >= 0) & (ranks[None, :] < ranks[:, None])
        best = lax.optimization_barrier(jnp.max(jnp.where(mask, similar, -1.0), axis=1))
        target = jnp.where(valid, index, total).astype(jnp.int32)
        return (target, best)
    targets, bests = lax.map(one_cluster, jnp.arange(CLUSTERS, dtype=jnp.int32))
    result = jnp.full((total,), -1.0, jnp.float32)
    return result.at[targets.reshape(-1)].set(bests.reshape(-1), mode='drop')
```

```python
import functools

import jax
import jax.numpy as jnp
from jax import lax
from jax.experimental import pallas as pl
from jax.experimental.pallas import tpu as pltpu
from jax.sharding import PartitionSpec as P

EMPTY = 1e9
VMEM_LIMIT = 48 * 1024 * 1024


def _nt(a, b):
    return lax.dot_general(a, b, (((1,), (1,)), ((), ())), preferred_element_type=jnp.float32)


def _slot_rows(lab, pos, dest, slots):
    key = jnp.where(lab == dest, pos, -1)
    places = lax.broadcasted_iota(jnp.int32, (slots, lab.shape[1]), 0)
    return (places == key).astype(jnp.float32).astype(jnp.bfloat16)


def _pack_first(partners, groups, slots, me_ref, emb_ref, lab_ref, prio_ref, unit_ref, pos_ref, ranks_ref, *outs):
    rows = emb_ref.shape[0]
    lab = lab_ref[...]
    onehot = (lax.broadcasted_iota(jnp.int32, (groups, rows), 0) == lab).astype(jnp.float32)
    before = lax.broadcasted_iota(jnp.int32, (rows, rows), 0) < lax.broadcasted_iota(jnp.int32, (rows, rows), 1)
    earlier = jnp.dot(
        onehot.astype(jnp.bfloat16),
        before.astype(jnp.float32).astype(jnp.bfloat16),
        preferred_element_type=jnp.float32,
    )
    pos = jnp.sum(onehot * earlier, axis=0, keepdims=True).astype(jnp.int32)
    pos_ref[...] = pos
    emb = emb_ref[...].astype(jnp.float32)
    unit = (emb * lax.rsqrt(jnp.sum(emb * emb, axis=1, keepdims=True) + 1e-06)).astype(jnp.bfloat16)
    unit_ref[...] = unit
    for partner, out in zip(partners, outs):
        pick = _slot_rows(lab, pos, jnp.bitwise_xor(me_ref[0], partner), slots)
        out[...] = jnp.dot(pick, unit, preferred_element_type=jnp.float32).astype(jnp.bfloat16)
    prio = prio_ref[...]
    high = (prio >> 8).astype(jnp.float32)
    low = (prio & 255).astype(jnp.float32)
    parts = jnp.concatenate([onehot * high, onehot * low, onehot], axis=0).astype(jnp.bfloat16)
    places = lax.broadcasted_iota(jnp.int32, (slots, rows), 0)
    placed = _nt(parts, (places == pos).astype(jnp.float32).astype(jnp.bfloat16))
    rank = placed[:groups] * 256.0 + placed[groups : 2 * groups]
    ranks_ref[...] = jnp.where(placed[2 * groups :] > 0.5, rank, EMPTY)


def _pack_rest(partners, slots, me_ref, unit_ref, lab_ref, pos_ref, *outs):
    for partner, out in zip(partners, outs):
        pick = _slot_rows(lab_ref[...], pos_ref[...], jnp.bitwise_xor(me_ref[0], partner), slots)
        out[...] = jnp.dot(pick, unit_ref[...], preferred_element_type=jnp.float32).astype(jnp.bfloat16)


def _score(order, n_old, slots, me_ref, own_ranks_ref, sib_ranks_ref, prev_ref, *rest):
    n = len(order)
    own, sib = rest[:n], rest[n : 2 * n]
    out_ref, q_scr, k_scr, q_rank, k_rank, sems = rest[2 * n :]
    copies = []
    for j in range(n):
        spans = [
            (own[j], k_scr.at[pl.ds(2 * j * slots, slots)]),
            (sib[j], k_scr.at[pl.ds((2 * j + 1) * slots, slots)]),
            (own[j], q_scr.at[pl.ds(j * slots, slots)]),
        ]
        for i, (src, dst) in enumerate(spans):
            if i < 2 or n_old < n:
                copy = pltpu.make_async_copy(src, dst, sems.at[j, i])
                copy.start()
                copies.append(copy)
    for j in range(n):
        source = jnp.bitwise_xor(me_ref[0], order[j])
        q_rank[pl.ds(j, 1), :] = own_ranks_ref[pl.ds(source, 1), :]
        k_rank[pl.ds(2 * j, 1), :] = own_ranks_ref[pl.ds(source, 1), :]
        k_rank[pl.ds(2 * j + 1, 1), :] = sib_ranks_ref[pl.ds(source, 1), :]
    k_col = jnp.transpose(k_rank[...])
    key_col = jnp.concatenate([k_col[:, j : j + 1] for j in range(2 * n)], axis=0)
    query_row = jnp.concatenate([q_rank[j : j + 1, :] for j in range(n)], axis=1)
    for copy in copies:
        copy.wait()

    def best_of(keys, queries):
        sim = _nt(k_scr[keys[0] * slots : keys[1] * slots, :], q_scr[queries[0] * slots : queries[1] * slots, :])
        mask = key_col[keys[0] * slots : keys[1] * slots] < query_row[:, queries[0] * slots : queries[1] * slots]
        return jnp.max(jnp.where(mask, sim, -1.0), axis=0, keepdims=True)

    rows = []
    if n_old:
        old = best_of((2 * n_old, 2 * n), (0, n_old))
        rows += [jnp.maximum(old[:, j * slots : (j + 1) * slots], prev_ref[j : j + 1, :]) for j in range(n_old)]
    new = best_of((0, 2 * n), (n_old, n))
    rows += [new[:, j * slots : (j + 1) * slots] for j in range(n - n_old)]
    last = n == out_ref.shape[0]
    for j in range(n):
        if last:
            out_ref[pl.ds(jnp.bitwise_xor(me_ref[0], order[j]), 1), :] = rows[j]
        else:
            out_ref[pl.ds(j, 1), :] = rows[j]


def _select(groups, lab_ref, pos_ref, got_ref, out_ref):
    slots = got_ref.shape[1]
    rows = lab_ref.shape[1]
    got = got_ref[...]
    a = got.astype(jnp.bfloat16)
    rest = got - a.astype(jnp.float32)
    b = rest.astype(jnp.bfloat16)
    c = (rest - b.astype(jnp.float32)).astype(jnp.bfloat16)
    places = lax.broadcasted_iota(jnp.int32, (slots, rows), 0)
    pick = (places == pos_ref[...]).astype(jnp.float32).astype(jnp.bfloat16)
    value = jnp.dot(a, pick, preferred_element_type=jnp.float32)
    value += jnp.dot(b, pick, preferred_element_type=jnp.float32)
    value += jnp.dot(c, pick, preferred_element_type=jnp.float32)
    mine = lax.broadcasted_iota(jnp.int32, (groups, rows), 0) == lab_ref[...]
    out_ref[...] = jnp.sum(jnp.where(mine, value, 0.0), axis=0, keepdims=True)


SMEM = pl.BlockSpec(memory_space=pltpu.SMEM)
VMEM = pl.BlockSpec(memory_space=pltpu.VMEM)
ANY = pl.BlockSpec(memory_space=pl.ANY)


def local(embeddings, labels, priority):
    rows, width = embeddings.shape
    groups = lax.axis_size("wide")
    slots = 2 * rows // groups
    half = groups // 2
    me = lax.axis_index("wide").astype(jnp.int32).reshape(1)
    lab = labels.reshape(1, rows)
    block = jax.ShapeDtypeStruct((slots, width), jnp.bfloat16)
    far, near = tuple(range(half, groups)), tuple(range(half))
    params = pltpu.CompilerParams(vmem_limit_bytes=VMEM_LIMIT)

    unit, pos, ranks, *far_blocks = pl.pallas_call(
        functools.partial(_pack_first, far, groups, slots),
        out_shape=[
            jax.ShapeDtypeStruct((rows, width), jnp.bfloat16),
            jax.ShapeDtypeStruct((1, rows), jnp.int32),
            jax.ShapeDtypeStruct((groups, slots), jnp.float32),
        ]
        + [block] * len(far),
        in_specs=[SMEM, VMEM, VMEM, VMEM],
        out_specs=[VMEM] * (3 + len(far)),
        compiler_params=params,
        name="pack_far",
    )(me, embeddings, lab, priority.reshape(1, rows))
    near_blocks = pl.pallas_call(
        functools.partial(_pack_rest, near, slots),
        out_shape=[block] * len(near),
        in_specs=[SMEM, VMEM, VMEM, VMEM],
        out_specs=[VMEM] * len(near),
        compiler_params=params,
        name="pack_near",
    )(me, unit, lab, pos)

    def swap(x):
        return lax.ppermute(x, "narrow", [(0, 1), (1, 0)])

    sent = dict(zip(far, far_blocks)) | dict(zip(near, near_blocks))
    own = {
        r: sent[r] if r == 0 else lax.ppermute(sent[r], "wide", [(s, s ^ r) for s in range(groups)])
        for r in far + near
    }
    own_ranks = lax.all_to_all(ranks, "wide", split_axis=0, concat_axis=0, tiled=True)
    sib_ranks = swap(own_ranks)
    sib = {r: swap(own[r]) for r in near + far}

    quarter = max(1, half // 4)
    steps = [near] + [far[i : i + quarter] for i in range(0, half, quarter)]
    order, best = (), jnp.zeros((groups, slots), jnp.float32)
    for step in steps:
        n_old = len(order)
        order = order + step
        n = len(order)
        best = pl.pallas_call(
            functools.partial(_score, order, n_old, slots),
            out_shape=jax.ShapeDtypeStruct((groups, slots), jnp.float32),
            in_specs=[SMEM, VMEM, VMEM, VMEM] + [ANY] * (2 * n),
            out_specs=VMEM,
            scratch_shapes=[
                pltpu.VMEM((n * slots, width), jnp.bfloat16),
                pltpu.VMEM((2 * n * slots, width), jnp.bfloat16),
                pltpu.VMEM((groups, slots), jnp.float32),
                pltpu.VMEM((2 * groups, slots), jnp.float32),
                pltpu.SemaphoreType.DMA((n, 3)),
            ],
            compiler_params=params,
            cost_estimate=pl.CostEstimate(
                flops=2 * width * slots * slots * 2 * (n_old * (n - n_old) + (n - n_old) * n),
                bytes_accessed=2 * n * slots * width * 2,
                transcendentals=0,
            ),
            name=f"score_{n}",
        )(me, own_ranks, sib_ranks, best, *[own[r] for r in order], *[sib[r] for r in order])

    returned = lax.all_to_all(best, "wide", split_axis=0, concat_axis=0, tiled=True)
    result = pl.pallas_call(
        functools.partial(_select, groups),
        out_shape=jax.ShapeDtypeStruct((1, rows), jnp.float32),
        in_specs=[VMEM, VMEM, VMEM],
        out_specs=VMEM,
        compiler_params=params,
        name="select",
    )(lab, pos, returned)
    return result.reshape(rows)


def solution(mesh):
    in_specs = (
        P(("parts", "wide", "narrow"), None),
        P(("parts", "wide", "narrow"), None),
        P(("parts", "wide", "narrow")),
    )
    out_specs = P(("parts", "wide", "narrow"))
    return jax.shard_map(local, mesh=mesh, in_specs=in_specs, out_specs=out_specs, check_vma=False)
```

```python
import functools

import jax
import jax.numpy as jnp
from jax import lax
from jax.experimental import pallas as pl
from jax.experimental.pallas import tpu as pltpu
from jax.sharding import PartitionSpec as P

EMPTY = 2.0**22
VMEM_LIMIT = 40 * 1024 * 1024
LANES = 128
TAIL = 16


def _nt(a, b):
    return lax.dot_general(a, b, (((1,), (1,)), ((), ())), preferred_element_type=jnp.float32)


def _as_bf16(mask):
    return mask.astype(jnp.float32).astype(jnp.bfloat16)


def _spans(slots):
    return -(-slots // LANES)


def _write_block(out, pick, unit, high, low, slots):
    block = jnp.dot(pick, unit, preferred_element_type=jnp.float32).astype(jnp.bfloat16)
    pieces = block.shape[1] // LANES
    for k in range(pieces):
        out[k * slots : (k + 1) * slots, :] = block[:, k * LANES : (k + 1) * LANES]
    spans = _spans(slots)
    lines = [part[:, i * LANES : (i + 1) * LANES] for part in (high, low) for i in range(spans)]
    lines.append(jnp.zeros((TAIL - 2 * spans, LANES), jnp.float32))
    out[pieces * slots :, :] = jnp.concatenate(lines, axis=0).astype(jnp.bfloat16)


def _block(ref, slots):
    return jnp.concatenate([ref[k * slots : (k + 1) * slots, :] for k in range(ref.shape[0] // slots)], axis=1)


def _ranks(ref, slots):
    tail = ref[ref.shape[0] - TAIL :, :].astype(jnp.float32)
    spans = _spans(slots)
    value = tail[:spans] * 256.0 + tail[spans : 2 * spans]
    return jnp.concatenate([value[i : i + 1] for i in range(spans)], axis=1)


def _pick(lab, pos, dest, slots):
    key = jnp.where(lab == dest, pos, -1)
    return _as_bf16(lax.broadcasted_iota(jnp.int32, (slots, lab.shape[1]), 0) == key)


def _pack_first(partners, groups, slots, me_ref, emb_ref, lab_ref, prio_ref, unit_ref, pos_ref, ranks_ref, *outs):
    rows = emb_ref.shape[0]
    lab = lab_ref[...]
    away = jnp.bitwise_xor(lax.broadcasted_iota(jnp.int32, (groups, rows), 0), me_ref[0])
    onehot = (away == lab).astype(jnp.float32)
    before = lax.broadcasted_iota(jnp.int32, (rows, rows), 0) < lax.broadcasted_iota(jnp.int32, (rows, rows), 1)
    earlier = jnp.dot(onehot.astype(jnp.bfloat16), _as_bf16(before), preferred_element_type=jnp.float32)
    pos = jnp.sum(onehot * earlier, axis=0, keepdims=True).astype(jnp.int32)
    pos_ref[...] = pos
    prio = prio_ref[...]
    high = (prio >> 8).astype(jnp.float32)
    low = (prio & 255).astype(jnp.float32)
    parts = jnp.concatenate([onehot * high, onehot * low, onehot], axis=0).astype(jnp.bfloat16)
    places = lax.broadcasted_iota(jnp.int32, (_spans(slots) * LANES, rows), 0)
    placed = _nt(parts, _as_bf16(places == pos))
    high = jnp.where(placed[2 * groups :] > 0.5, placed[:groups], EMPTY)
    low = placed[groups : 2 * groups]
    ranks_ref[...] = jnp.concatenate([high, low], axis=0)
    emb = emb_ref[...].astype(jnp.float32)
    unit = (emb * lax.rsqrt(jnp.sum(emb * emb, axis=1, keepdims=True) + 1e-06)).astype(jnp.bfloat16)
    unit_ref[...] = unit
    for partner, out in zip(partners, outs):
        pick = _pick(lab, pos, jnp.bitwise_xor(me_ref[0], partner), slots)
        _write_block(out, pick, unit, high[partner : partner + 1], low[partner : partner + 1], slots)


def _pack_rest(partners, groups, slots, me_ref, unit_ref, lab_ref, pos_ref, ranks_ref, *outs):
    for partner, out in zip(partners, outs):
        pick = _pick(lab_ref[...], pos_ref[...], jnp.bitwise_xor(me_ref[0], partner), slots)
        high = ranks_ref[partner : partner + 1, :]
        low = ranks_ref[groups + partner : groups + partner + 1, :]
        _write_block(out, pick, unit_ref[...], high, low, slots)


def _score(order, n_old, slots, me_ref, prev_ref, *rest):
    n = len(order)
    own, sib, out_ref = rest[:n], rest[n : 2 * n], rest[2 * n]
    refs = [ref for j in range(n) for ref in (own[j], sib[j])]
    ranks = jnp.concatenate([_ranks(ref, slots) for ref in refs], axis=0)
    columns = jnp.transpose(ranks)[:slots]

    def best_of(keys, queries):
        sim = _nt(
            jnp.concatenate([_block(refs[i], slots) for i in keys], axis=0),
            jnp.concatenate([_block(own[j], slots) for j in queries], axis=0),
        )
        key_ranks = jnp.concatenate([columns[:, i : i + 1] for i in keys], axis=0)
        query_ranks = jnp.concatenate([ranks[2 * j : 2 * j + 1, :slots] for j in queries], axis=1)
        best = jnp.max(jnp.where(key_ranks < query_ranks, sim, -1.0), axis=0, keepdims=True)
        return [best[:, i * slots : (i + 1) * slots] for i in range(len(queries))]

    rows = []
    if n_old:
        old = best_of(range(2 * n_old, 2 * n), range(n_old))
        rows += [jnp.maximum(old[j], prev_ref[j : j + 1, :]) for j in range(n_old)]
    rows += best_of(range(2 * n), range(n_old, n))
    last = n == out_ref.shape[0]
    for j in range(n):
        if last:
            out_ref[pl.ds(jnp.bitwise_xor(me_ref[0], order[j]), 1), :] = rows[j]
        else:
            out_ref[pl.ds(j, 1), :] = rows[j]


def _select(groups, lab_ref, pos_ref, got_ref, out_ref):
    slots = got_ref.shape[1]
    rows = lab_ref.shape[1]
    got = got_ref[...]
    a = got.astype(jnp.bfloat16)
    rest = got - a.astype(jnp.float32)
    b = rest.astype(jnp.bfloat16)
    c = (rest - b.astype(jnp.float32)).astype(jnp.bfloat16)
    pick = _as_bf16(lax.broadcasted_iota(jnp.int32, (slots, rows), 0) == pos_ref[...])
    value = jnp.dot(a, pick, preferred_element_type=jnp.float32)
    value += jnp.dot(b, pick, preferred_element_type=jnp.float32)
    value += jnp.dot(c, pick, preferred_element_type=jnp.float32)
    mine = lax.broadcasted_iota(jnp.int32, (groups, rows), 0) == lab_ref[...]
    out_ref[...] = jnp.sum(jnp.where(mine, value, 0.0), axis=0, keepdims=True)


SMEM = pl.BlockSpec(memory_space=pltpu.SMEM)
VMEM = pl.BlockSpec(memory_space=pltpu.VMEM)


def local(embeddings, labels, priority):
    rows, width = embeddings.shape
    groups = lax.axis_size("wide")
    slots = 2 * rows // groups
    half = groups // 2
    me = lax.axis_index("wide").astype(jnp.int32).reshape(1)
    lab = labels.reshape(1, rows)
    block = jax.ShapeDtypeStruct((width // LANES * slots + TAIL, LANES), jnp.bfloat16)
    far, near = tuple(range(half, groups)), tuple(range(half))
    params = pltpu.CompilerParams(vmem_limit_bytes=VMEM_LIMIT)

    unit, pos, ranks, *far_blocks = pl.pallas_call(
        functools.partial(_pack_first, far, groups, slots),
        out_shape=[
            jax.ShapeDtypeStruct((rows, width), jnp.bfloat16),
            jax.ShapeDtypeStruct((1, rows), jnp.int32),
            jax.ShapeDtypeStruct((2 * groups, _spans(slots) * LANES), jnp.float32),
        ]
        + [block] * len(far),
        in_specs=[SMEM, VMEM, VMEM, VMEM],
        out_specs=[VMEM] * (3 + len(far)),
        compiler_params=params,
        name="pack_far",
    )(me, embeddings, lab, priority.reshape(1, rows))
    near_blocks = pl.pallas_call(
        functools.partial(_pack_rest, near, groups, slots),
        out_shape=[block] * len(near),
        in_specs=[SMEM] + [VMEM] * 4,
        out_specs=[VMEM] * len(near),
        compiler_params=params,
        name="pack_near",
    )(me, unit, lab, pos, ranks)

    def swap(x):
        return lax.ppermute(x, "narrow", [(0, 1), (1, 0)])

    def send(x, r):
        return lax.ppermute(x, "wide", [(s, s ^ r) for s in range(groups)])

    def after(x, *others):
        return lax.optimization_barrier((x, *others))[0]

    own = {}
    for i, r in enumerate(far):
        out = far_blocks[i]
        dep = {6: (4, 5), 7: (4, 5)}.get(r)
        if dep is not None:
            out = after(out, *[own[d] for d in dep])
        own[r] = send(out, r)
    for i, r in enumerate(near):
        dep = {}.get(r)
        out = near_blocks[i] if dep is None else after(near_blocks[i], own[dep])
        own[r] = send(out, r) if r else out

    steps = [(0,1,2,3,4,5),(6,),(7,)]
    order, best, sib = (), jnp.zeros((groups, slots), jnp.float32), {}
    for step in steps:
        for r in step:
            sib[r] = swap(after(own[r], best) if r in (7,) else own[r])
        n_old = len(order)
        order = order + step
        n = len(order)
        best = pl.pallas_call(
            functools.partial(_score, order, n_old, slots),
            out_shape=jax.ShapeDtypeStruct((groups, slots), jnp.float32),
            in_specs=[SMEM] + [VMEM] * (1 + 2 * n),
            out_specs=VMEM,
            compiler_params=params,
            cost_estimate=pl.CostEstimate(
                flops=2 * width * slots * slots * 2 * (n_old * (n - n_old) + (n - n_old) * n),
                bytes_accessed=2 * n * slots * width * 2,
                transcendentals=0,
            ),
            name=f"score_{n}",
        )(me, best, *[own[r] for r in order], *[sib[r] for r in order])

    returned = lax.all_to_all(best, "wide", split_axis=0, concat_axis=0, tiled=True)
    result = pl.pallas_call(
        functools.partial(_select, groups),
        out_shape=jax.ShapeDtypeStruct((1, rows), jnp.float32),
        in_specs=[VMEM, VMEM, VMEM],
        out_specs=VMEM,
        compiler_params=params,
        name="select",
    )(lab, pos, returned)
    return result.reshape(rows)


def solution(mesh):
    in_specs = (
        P(("parts", "wide", "narrow"), None),
        P(("parts", "wide", "narrow"), None),
        P(("parts", "wide", "narrow")),
    )
    out_specs = P(("parts", "wide", "narrow"))
    return jax.shard_map(local, mesh=mesh, in_specs=in_specs, out_specs=out_specs, check_vma=False)
```

```python
import functools

import jax
import jax.numpy as jnp
from jax import lax
from jax.experimental import pallas as pl
from jax.experimental.pallas import tpu as pltpu
from jax.sharding import PartitionSpec as P

EMPTY = 2.0**22
VMEM_LIMIT = 40 * 1024 * 1024
LANES = 128
CHUNKS = 4
SPLIT = 1024
TAIL = 16


def _nt(a, b):
    return lax.dot_general(a, b, (((1,), (1,)), ((), ())), preferred_element_type=jnp.float32)


def _as_bf16(mask):
    return mask.astype(jnp.float32).astype(jnp.bfloat16)


def _spans(slots):
    return -(-slots // LANES)


def _write_block(out, pick, unit, high, low, slots):
    block = jnp.dot(pick, unit, preferred_element_type=jnp.float32).astype(jnp.bfloat16)
    pieces = block.shape[1] // LANES
    for k in range(pieces):
        out[k * slots : (k + 1) * slots, :] = block[:, k * LANES : (k + 1) * LANES]
    spans = _spans(slots)
    lines = [part[:, i * LANES : (i + 1) * LANES] for part in (high, low) for i in range(spans)]
    lines.append(jnp.zeros((TAIL - 2 * spans, LANES), jnp.float32))
    out[pieces * slots :, :] = jnp.concatenate(lines, axis=0).astype(jnp.bfloat16)


def _block(ref, slots):
    return jnp.concatenate([ref[k * slots : (k + 1) * slots, :] for k in range(ref.shape[0] // slots)], axis=1)


def _ranks(ref, slots):
    tail = ref[ref.shape[0] - TAIL :, :].astype(jnp.float32)
    spans = _spans(slots)
    value = tail[:spans] * 256.0 + tail[spans : 2 * spans]
    return jnp.concatenate([value[i : i + 1] for i in range(spans)], axis=1)


def _pick(lab, pos, dest, low, high):
    key = jnp.where(lab == dest, pos, -1)
    return _as_bf16(lax.broadcasted_iota(jnp.int32, (high - low, lab.shape[1]), 0) + low == key)


def _pack_first(pieces, groups, slots, me_ref, emb_hbm, lab_hbm, prio_hbm, *rest):
    unit_ref, pos_ref, ranks_ref, *outs = rest[:-5]
    emb_ref, lab_ref, prio_ref, sems, word_sems = rest[-5:]
    rows = emb_ref.shape[0]
    words = [
        pltpu.make_async_copy(lab_hbm, lab_ref, word_sems.at[0]),
        pltpu.make_async_copy(prio_hbm, prio_ref, word_sems.at[1]),
    ]
    chunk = rows // CHUNKS
    spans = [pl.ds(i * chunk, chunk) for i in range(CHUNKS)]
    copies = [pltpu.make_async_copy(emb_hbm.at[span], emb_ref.at[span], sems.at[i]) for i, span in enumerate(spans)]
    for copy in words + copies:
        copy.start()
    for copy in words:
        copy.wait()
    lab = lab_ref[...]
    away = jnp.bitwise_xor(lax.broadcasted_iota(jnp.int32, (groups, rows), 0), me_ref[0])
    onehot = (away == lab).astype(jnp.float32)
    before = lax.broadcasted_iota(jnp.int32, (rows, rows), 0) < lax.broadcasted_iota(jnp.int32, (rows, rows), 1)
    earlier = jnp.dot(onehot.astype(jnp.bfloat16), _as_bf16(before), preferred_element_type=jnp.float32)
    pos = jnp.sum(onehot * earlier, axis=0, keepdims=True).astype(jnp.int32)
    pos_ref[...] = pos
    prio = jnp.concatenate([prio_ref[i : i + 1, :] for i in range(rows // LANES)], axis=1)
    high = (prio >> 8).astype(jnp.float32)
    low = (prio & 255).astype(jnp.float32)
    parts = jnp.concatenate([onehot * high, onehot * low, onehot], axis=0).astype(jnp.bfloat16)
    places = lax.broadcasted_iota(jnp.int32, (_spans(slots) * LANES, rows), 0)
    placed = _nt(parts, _as_bf16(places == pos))
    high = jnp.where(placed[2 * groups :] > 0.5, placed[:groups], EMPTY)
    low = placed[groups : 2 * groups]
    ranks_ref[...] = jnp.concatenate([high, low], axis=0)
    for copy, span in zip(copies, spans):
        copy.wait()
        emb = emb_ref[span, :].astype(jnp.float32)
        scale = lax.rsqrt(jnp.sum(emb * emb, axis=1, keepdims=True) + 1e-06)
        unit_ref[span, :] = (emb * scale).astype(jnp.bfloat16)
    unit = unit_ref[...]
    for (r, first, last), out in zip(pieces, outs):
        pick = _pick(lab, pos, jnp.bitwise_xor(me_ref[0], r), first, last)
        _write_block(out, pick, unit, high[r : r + 1, first:], low[r : r + 1, first:], last - first)


def _pack_rest(pieces, groups, me_ref, unit_ref, lab_ref, pos_ref, ranks_ref, after_ref, *outs):
    for (r, first, last), out in zip(pieces, outs):
        pick = _pick(lab_ref[...], pos_ref[...], jnp.bitwise_xor(me_ref[0], r), first, last)
        high = ranks_ref[r : r + 1, first:]
        low = ranks_ref[groups + r : groups + r + 1, first:]
        _write_block(out, pick, unit_ref[...], high, low, last - first)


def _score(pieces, n_old, final, me_ref, prev_ref, *rest):
    n = len(pieces)
    own, sib, out_ref = rest[:n], rest[n : 2 * n], rest[2 * n]
    sizes = [last - first for _, first, last in pieces]
    refs = [ref for j in range(n) for ref in (own[j], sib[j])]
    ranks = [_ranks(ref, sizes[i // 2]) for i, ref in enumerate(refs)]
    lanes = max(rank.shape[1] for rank in ranks)
    padded = [jnp.concatenate([rank] * (lanes // rank.shape[1]), axis=1) for rank in ranks]
    columns = jnp.transpose(jnp.concatenate(padded, axis=0))

    def best_of(keys, queries):
        sim = _nt(
            jnp.concatenate([_block(refs[i], sizes[i // 2]) for i in keys], axis=0),
            jnp.concatenate([_block(own[j], sizes[j]) for j in queries], axis=0),
        )
        key_ranks = jnp.concatenate([columns[: sizes[i // 2], i : i + 1] for i in keys], axis=0)
        query_ranks = jnp.concatenate([ranks[2 * j][:, : sizes[j]] for j in queries], axis=1)
        best = jnp.max(jnp.where(key_ranks < query_ranks, sim, -1.0), axis=0, keepdims=True)
        starts = [sum(sizes[j] for j in queries[:i]) for i in range(len(queries) + 1)]
        return [best[:, starts[i] : starts[i + 1]] for i in range(len(queries))]

    rows = []
    if n_old:
        old = best_of(range(2 * n_old, 2 * n), range(n_old))
        for (r, first, last), row in zip(pieces, old):
            rows.append(jnp.maximum(row, prev_ref[r : r + 1, first:last]))
    rows += best_of(range(2 * n), range(n_old, n))
    if not final:
        for (r, first, last), row in zip(pieces, rows):
            out_ref[r : r + 1, first:last] = row
    else:
        for r in range(out_ref.shape[0]):
            whole = [row for piece, row in sorted(zip(pieces, rows), key=lambda pair: pair[0]) if piece[0] == r]
            out_ref[pl.ds(jnp.bitwise_xor(me_ref[0], r), 1), :] = jnp.concatenate(whole, axis=1)


def _select(groups, lab_ref, pos_ref, got_ref, out_ref):
    slots = got_ref.shape[1]
    rows = lab_ref.shape[1]
    got = got_ref[...]
    a = got.astype(jnp.bfloat16)
    rest = got - a.astype(jnp.float32)
    b = rest.astype(jnp.bfloat16)
    c = (rest - b.astype(jnp.float32)).astype(jnp.bfloat16)
    pick = _as_bf16(lax.broadcasted_iota(jnp.int32, (slots, rows), 0) == pos_ref[...])
    value = jnp.dot(a, pick, preferred_element_type=jnp.float32)
    value += jnp.dot(b, pick, preferred_element_type=jnp.float32)
    value += jnp.dot(c, pick, preferred_element_type=jnp.float32)
    mine = lax.broadcasted_iota(jnp.int32, (groups, rows), 0) == lab_ref[...]
    out_ref[...] = jnp.sum(jnp.where(mine, value, 0.0), axis=0)


ANY = pl.BlockSpec(memory_space=pl.ANY)
SMEM = pl.BlockSpec(memory_space=pltpu.SMEM)
VMEM = pl.BlockSpec(memory_space=pltpu.VMEM)
HBM = pl.BlockSpec(memory_space=pltpu.HBM)


def local(embeddings, labels, priority):
    rows, width = embeddings.shape
    groups = lax.axis_size("wide")
    slots = 2 * rows // groups
    half = groups // 2
    me = lax.axis_index("wide").astype(jnp.int32).reshape(1)
    lab = labels.reshape(1, rows)
    def block(piece):
        return jax.ShapeDtypeStruct((width // LANES * (piece[2] - piece[1]) + TAIL, LANES), jnp.bfloat16)

    quarter = max(1, half // 4)
    near = [(r, 0, slots) for r in range(half)]
    far = [(r, 0, slots) for r in range(half, groups)]
    if SPLIT < slots:
        far[-1:] = [(groups - 1, 0, SPLIT), (groups - 1, SPLIT, slots)]
    params = pltpu.CompilerParams(vmem_limit_bytes=VMEM_LIMIT)

    def in_hbm(x):
        return pltpu.with_memory_space_constraint(x, pltpu.HBM)

    unit, pos, ranks, *far_blocks = pl.pallas_call(
        functools.partial(_pack_first, far, groups, slots),
        out_shape=[
            jax.ShapeDtypeStruct((rows, width), jnp.bfloat16),
            jax.ShapeDtypeStruct((1, rows), jnp.int32),
            jax.ShapeDtypeStruct((2 * groups, _spans(slots) * LANES), jnp.float32),
        ]
        + [block(piece) for piece in far],
        in_specs=[SMEM, HBM, HBM, HBM],
        out_specs=[VMEM] * (3 + len(far)),
        scratch_shapes=[
            pltpu.VMEM((rows, width), jnp.bfloat16),
            pltpu.VMEM((1, rows), jnp.int32),
            pltpu.VMEM((rows // LANES, LANES), jnp.int32),
            pltpu.SemaphoreType.DMA((CHUNKS,)),
            pltpu.SemaphoreType.DMA((2,)),
        ],
        compiler_params=params,
        name="pack_far",
    )(me, in_hbm(embeddings), in_hbm(lab), in_hbm(priority.reshape(rows // LANES, LANES)))
    def swap(x):
        return lax.ppermute(x, "narrow", [(0, 1), (1, 0)])

    def send(x, r):
        return lax.ppermute(x, "wide", [(s, s ^ r) for s in range(groups)])

    def after(x, *others):
        return lax.optimization_barrier((x, *others))[0]

    near_blocks = pl.pallas_call(
        functools.partial(_pack_rest, near, groups),
        out_shape=[block(piece) for piece in near],
        in_specs=[SMEM] + [VMEM] * 4 + [ANY],
        out_specs=[VMEM] * len(near),
        compiler_params=params,
        cost_estimate=pl.CostEstimate(flops=10000000000, bytes_accessed=1, transcendentals=0),
        name="pack_near",
    )(me, unit, lab, pos, ranks, ranks)

    own = {}
    for i, piece in enumerate(far):
        out = far_blocks[i]
        if i >= 2 * quarter:
            out = after(out, own[far[i - 2 * quarter]])
        own[piece] = send(out, piece[0])
    for piece, out in zip(near, near_blocks):
        own[piece] = send(out, piece[0]) if piece[0] else out

    steps = [
        near[:1] + far[:quarter],
        far[quarter : 2 * quarter] + near[1:],
        far[2 * quarter : 3 * quarter],
        far[3 * quarter : 4 * quarter],
        far[4 * quarter :],
    ]
    steps = [step for step in steps if step]
    order, best, sib = [], jnp.zeros((groups, slots), jnp.float32), {}
    for number, step in enumerate(steps):
        for piece in step:
            sib[piece] = swap(after(own[piece], best) if number >= 3 else own[piece])
        n_old = len(order)
        order = order + step
        old, new = (sum(piece[2] - piece[1] for piece in part) for part in (order[:n_old], step))
        best = pl.pallas_call(
            functools.partial(_score, order, n_old, number == len(steps) - 1),
            out_shape=jax.ShapeDtypeStruct((groups, slots), jnp.float32),
            in_specs=[SMEM] + [VMEM] * (1 + 2 * len(order)),
            out_specs=VMEM,
            compiler_params=params,
            cost_estimate=pl.CostEstimate(
                flops=10000000000,
                bytes_accessed=4 * (old + new) * width,
                transcendentals=0,
            ),
            name=f"score_{number}",
        )(me, best, *[own[piece] for piece in order], *[sib[piece] for piece in order])

    returned = lax.all_to_all(best, "wide", split_axis=0, concat_axis=0, tiled=True)
    return pl.pallas_call(
        functools.partial(_select, groups),
        out_shape=jax.ShapeDtypeStruct((rows,), jnp.float32),
        in_specs=[VMEM, VMEM, VMEM],
        out_specs=VMEM,
        compiler_params=params,
        name="select",
    )(lab, pos, returned)


def solution(mesh):
    in_specs = (
        P(("parts", "wide", "narrow"), None),
        P(("parts", "wide", "narrow"), None),
        P(("parts", "wide", "narrow")),
    )
    out_specs = P(("parts", "wide", "narrow"))
    return jax.shard_map(local, mesh=mesh, in_specs=in_specs, out_specs=out_specs, check_vma=False)
```

```python
import functools

import jax
import jax.numpy as jnp
from jax import lax
from jax.experimental import pallas as pl
from jax.experimental.pallas import tpu as pltpu
from jax.sharding import PartitionSpec as P

EMPTY = 2.0**22
VMEM_LIMIT = 40 * 1024 * 1024
LANES = 128
CHUNKS = 4
COSTS = (10000000000, 30000000000, 1, 1)
HALVES = (2,)
SPLIT = 1024
TAIL = 16


def _nt(a, b):
    return lax.dot_general(a, b, (((1,), (1,)), ((), ())), preferred_element_type=jnp.float32)


def _as_bf16(mask):
    return mask.astype(jnp.float32).astype(jnp.bfloat16)


def _spans(slots):
    return -(-slots // LANES)


def _write_block(out, pick, unit, high, low, slots):
    block = jnp.dot(pick, unit, preferred_element_type=jnp.float32).astype(jnp.bfloat16)
    pieces = block.shape[1] // LANES
    for k in range(pieces):
        out[k * slots : (k + 1) * slots, :] = block[:, k * LANES : (k + 1) * LANES]
    spans = _spans(slots)
    lines = [part[:, i * LANES : (i + 1) * LANES] for part in (high, low) for i in range(spans)]
    lines.append(jnp.zeros((TAIL - 2 * spans, LANES), jnp.float32))
    out[pieces * slots :, :] = jnp.concatenate(lines, axis=0).astype(jnp.bfloat16)


def _block(parts, slots):
    pieces = [ref[k * slots : (k + 1) * slots, :] for ref in parts for k in range(ref.shape[0] // slots)]
    return jnp.concatenate(pieces, axis=1)


def _ranks(parts, slots):
    ref = parts[-1]
    tail = ref[ref.shape[0] - TAIL :, :].astype(jnp.float32)
    spans = _spans(slots)
    value = tail[:spans] * 256.0 + tail[spans : 2 * spans]
    return jnp.concatenate([value[i : i + 1] for i in range(spans)], axis=1)


def _pick(lab, pos, dest, low, high):
    key = jnp.where(lab == dest, pos, -1)
    return _as_bf16(lax.broadcasted_iota(jnp.int32, (high - low, lab.shape[1]), 0) + low == key)


def _pack_first(pieces, groups, slots, me_ref, emb_hbm, lab_hbm, prio_hbm, *rest):
    unit_ref, pos_ref, ranks_ref, *outs = rest[:-5]
    emb_ref, lab_ref, prio_ref, sems, word_sems = rest[-5:]
    rows = emb_ref.shape[0]
    words = [
        pltpu.make_async_copy(lab_hbm, lab_ref, word_sems.at[0]),
        pltpu.make_async_copy(prio_hbm, prio_ref, word_sems.at[1]),
    ]
    chunk = rows // CHUNKS
    spans = [pl.ds(i * chunk, chunk) for i in range(CHUNKS)]
    copies = [pltpu.make_async_copy(emb_hbm.at[span], emb_ref.at[span], sems.at[i]) for i, span in enumerate(spans)]
    for copy in words + copies:
        copy.start()
    for copy in words:
        copy.wait()
    lab = lab_ref[...]
    away = jnp.bitwise_xor(lax.broadcasted_iota(jnp.int32, (groups, rows), 0), me_ref[0])
    onehot = (away == lab).astype(jnp.float32)
    before = lax.broadcasted_iota(jnp.int32, (rows, rows), 0) < lax.broadcasted_iota(jnp.int32, (rows, rows), 1)
    earlier = jnp.dot(onehot.astype(jnp.bfloat16), _as_bf16(before), preferred_element_type=jnp.float32)
    pos = jnp.sum(onehot * earlier, axis=0, keepdims=True).astype(jnp.int32)
    pos_ref[...] = pos
    prio = jnp.concatenate([prio_ref[i : i + 1, :] for i in range(rows // LANES)], axis=1)
    high = (prio >> 8).astype(jnp.float32)
    low = (prio & 255).astype(jnp.float32)
    parts = jnp.concatenate([onehot * high, onehot * low, onehot], axis=0).astype(jnp.bfloat16)
    places = lax.broadcasted_iota(jnp.int32, (_spans(slots) * LANES, rows), 0)
    placed = _nt(parts, _as_bf16(places == pos))
    high = jnp.where(placed[2 * groups :] > 0.5, placed[:groups], EMPTY)
    low = placed[groups : 2 * groups]
    ranks_ref[...] = jnp.concatenate([high, low], axis=0)
    for copy, span in zip(copies, spans):
        copy.wait()
        emb = emb_ref[span, :].astype(jnp.float32)
        scale = lax.rsqrt(jnp.sum(emb * emb, axis=1, keepdims=True) + 1e-06)
        unit_ref[span, :] = (emb * scale).astype(jnp.bfloat16)
    unit = unit_ref[...]
    for (r, first, last), out in zip(pieces, outs):
        pick = _pick(lab, pos, jnp.bitwise_xor(me_ref[0], r), first, last)
        _write_block(out, pick, unit, high[r : r + 1, first:], low[r : r + 1, first:], last - first)


def _pack_rest(pieces, groups, me_ref, unit_ref, lab_ref, pos_ref, ranks_ref, *outs):
    for (r, first, last), out in zip(pieces, outs):
        pick = _pick(lab_ref[...], pos_ref[...], jnp.bitwise_xor(me_ref[0], r), first, last)
        high = ranks_ref[r : r + 1, first:]
        low = ranks_ref[groups + r : groups + r + 1, first:]
        _write_block(out, pick, unit_ref[...], high, low, last - first)


def _score(pieces, n_old, final, me_ref, prev_ref, *rest):
    n = len(pieces)
    out_ref, rest = rest[-1], list(rest[:-1])
    sizes = [last - first for _, first, last in pieces]
    blocks = []
    while rest:
        parts = [rest.pop(0)]
        whole = parts[0].shape[0] % sizes[len(blocks) % n] == TAIL
        blocks.append(parts if whole else parts + [rest.pop(0)])
    own, sib = blocks[:n], blocks[n:]
    refs = [ref for j in range(n) for ref in (own[j], sib[j])]
    ranks = [_ranks(ref, sizes[i // 2]) for i, ref in enumerate(refs)]
    lanes = max(rank.shape[1] for rank in ranks)
    padded = [jnp.concatenate([rank] * (lanes // rank.shape[1]), axis=1) for rank in ranks]
    columns = jnp.transpose(jnp.concatenate(padded, axis=0))

    def best_of(keys, queries):
        sim = _nt(
            jnp.concatenate([_block(refs[i], sizes[i // 2]) for i in keys], axis=0),
            jnp.concatenate([_block(own[j], sizes[j]) for j in queries], axis=0),
        )
        key_ranks = jnp.concatenate([columns[: sizes[i // 2], i : i + 1] for i in keys], axis=0)
        query_ranks = jnp.concatenate([ranks[2 * j][:, : sizes[j]] for j in queries], axis=1)
        best = jnp.max(jnp.where(key_ranks < query_ranks, sim, -1.0), axis=0, keepdims=True)
        starts = [sum(sizes[j] for j in queries[:i]) for i in range(len(queries) + 1)]
        return [best[:, starts[i] : starts[i + 1]] for i in range(len(queries))]

    rows = []
    if n_old:
        old = best_of(range(2 * n_old, 2 * n), range(n_old))
        for (r, first, last), row in zip(pieces, old):
            rows.append(jnp.maximum(row, prev_ref[r : r + 1, first:last]))
    rows += best_of(range(2 * n), range(n_old, n))
    if not final:
        for (r, first, last), row in zip(pieces, rows):
            out_ref[r : r + 1, first:last] = row
    else:
        for r in range(out_ref.shape[0]):
            whole = [row for piece, row in sorted(zip(pieces, rows), key=lambda pair: pair[0]) if piece[0] == r]
            out_ref[pl.ds(jnp.bitwise_xor(me_ref[0], r), 1), :] = jnp.concatenate(whole, axis=1)


def _select(groups, lab_ref, pos_ref, got_ref, out_ref):
    slots = got_ref.shape[1]
    rows = lab_ref.shape[1]
    got = got_ref[...]
    a = got.astype(jnp.bfloat16)
    rest = got - a.astype(jnp.float32)
    b = rest.astype(jnp.bfloat16)
    c = (rest - b.astype(jnp.float32)).astype(jnp.bfloat16)
    pick = _as_bf16(lax.broadcasted_iota(jnp.int32, (slots, rows), 0) == pos_ref[...])
    value = jnp.dot(a, pick, preferred_element_type=jnp.float32)
    value += jnp.dot(b, pick, preferred_element_type=jnp.float32)
    value += jnp.dot(c, pick, preferred_element_type=jnp.float32)
    mine = lax.broadcasted_iota(jnp.int32, (groups, rows), 0) == lab_ref[...]
    out_ref[...] = jnp.sum(jnp.where(mine, value, 0.0), axis=0)


SMEM = pl.BlockSpec(memory_space=pltpu.SMEM)
VMEM = pl.BlockSpec(memory_space=pltpu.VMEM)
HBM = pl.BlockSpec(memory_space=pltpu.HBM)


def local(embeddings, labels, priority):
    rows, width = embeddings.shape
    groups = lax.axis_size("wide")
    slots = 2 * rows // groups
    half = groups // 2
    me = lax.axis_index("wide").astype(jnp.int32).reshape(1)
    lab = labels.reshape(1, rows)
    def block(piece):
        return jax.ShapeDtypeStruct((width // LANES * (piece[2] - piece[1]) + TAIL, LANES), jnp.bfloat16)

    quarter = max(1, half // 4)
    near = [(r, 0, slots) for r in range(half)]
    far = [(r, 0, slots) for r in range(half, groups)]
    if SPLIT < slots:
        far[-1:] = [(groups - 1, 0, SPLIT), (groups - 1, SPLIT, slots)]
    params = pltpu.CompilerParams(vmem_limit_bytes=VMEM_LIMIT)

    def in_hbm(x):
        return pltpu.with_memory_space_constraint(x, pltpu.HBM)

    unit, pos, ranks, *far_blocks = pl.pallas_call(
        functools.partial(_pack_first, far[:quarter], groups, slots),
        out_shape=[
            jax.ShapeDtypeStruct((rows, width), jnp.bfloat16),
            jax.ShapeDtypeStruct((1, rows), jnp.int32),
            jax.ShapeDtypeStruct((2 * groups, _spans(slots) * LANES), jnp.float32),
        ]
        + [block(piece) for piece in far[:quarter]],
        in_specs=[SMEM, HBM, HBM, HBM],
        out_specs=[VMEM] * (3 + quarter),
        scratch_shapes=[
            pltpu.VMEM((rows, width), jnp.bfloat16),
            pltpu.VMEM((1, rows), jnp.int32),
            pltpu.VMEM((rows // LANES, LANES), jnp.int32),
            pltpu.SemaphoreType.DMA((CHUNKS,)),
            pltpu.SemaphoreType.DMA((2,)),
        ],
        compiler_params=params,
        name="pack_first",
    )(me, in_hbm(embeddings), in_hbm(lab), in_hbm(priority.reshape(rows // LANES, LANES)))
    def swap(x):
        return lax.ppermute(x, "narrow", [(0, 1), (1, 0)])

    def send(x, r):
        return lax.ppermute(x, "wide", [(s, s ^ r) for s in range(groups)])

    def after(x, *others):
        return lax.optimization_barrier((x, *others))[0]

    def pack_rest(pieces, name):
        return pl.pallas_call(
            functools.partial(_pack_rest, pieces, groups),
            out_shape=[block(piece) for piece in pieces],
            in_specs=[SMEM] + [VMEM] * 4,
            out_specs=[VMEM] * len(pieces),
            compiler_params=params,
            cost_estimate=pl.CostEstimate(flops=30000000000, bytes_accessed=1, transcendentals=0),
            name=name,
        )(me, unit, lab, pos, ranks)

    far_blocks += pack_rest(far[quarter:], "pack_far")
    near_blocks = pack_rest(near, "pack_near")
    own = {}
    for i, piece in enumerate(far):
        out = far_blocks[i]
        if i >= 2 * quarter:
            out = after(out, own[far[i - 2 * quarter]])
        own[piece] = send(out, piece[0])
    for piece, out in zip(near, near_blocks):
        own[piece] = send(out, piece[0]) if piece[0] else out

    steps = [
        near[:1] + far[:quarter],
        far[quarter : 2 * quarter] + near[1:],
        far[2 * quarter : 3 * quarter],
        far[3 * quarter : 4 * quarter],
        far[4 * quarter :],
    ]
    steps = [step for step in steps if step]
    order, best, sib = [], jnp.zeros((groups, slots), jnp.float32), {}
    for number, step in enumerate(steps):
        for piece in step:
            ready = after(own[piece], best) if number >= 2 else own[piece]
            cut = width // LANES // 2 * (piece[2] - piece[1])
            sib[piece] = [swap(part) for part in ((ready[:cut], ready[cut:]) if number in HALVES else (ready,))]
        n_old = len(order)
        order = order + step
        old, new = (sum(piece[2] - piece[1] for piece in part) for part in (order[:n_old], step))
        partners = [part for piece in order for part in sib[piece]]
        best = pl.pallas_call(
            functools.partial(_score, order, n_old, number == len(steps) - 1),
            out_shape=jax.ShapeDtypeStruct((groups, slots), jnp.float32),
            in_specs=[SMEM] + [VMEM] * (1 + len(order) + len(partners)),
            out_specs=VMEM,
            compiler_params=params,
            cost_estimate=pl.CostEstimate(
                flops=COSTS[number],
                bytes_accessed=1,
                transcendentals=0,
            ),
            name=f"score_{number}",
        )(me, best, *[own[piece] for piece in order], *partners)

    returned = lax.all_to_all(best, "wide", split_axis=0, concat_axis=0, tiled=True)
    return pl.pallas_call(
        functools.partial(_select, groups),
        out_shape=jax.ShapeDtypeStruct((rows,), jnp.float32),
        in_specs=[VMEM, VMEM, VMEM],
        out_specs=VMEM,
        compiler_params=params,
        name="select",
    )(lab, pos, returned)


def solution(mesh):
    in_specs = (
        P(("parts", "wide", "narrow"), None),
        P(("parts", "wide", "narrow"), None),
        P(("parts", "wide", "narrow")),
    )
    out_specs = P(("parts", "wide", "narrow"))
    return jax.shard_map(local, mesh=mesh, in_specs=in_specs, out_specs=out_specs, check_vma=False)
```

```python
import functools

import jax
import jax.numpy as jnp
from jax import lax
from jax.experimental import pallas as pl
from jax.experimental.pallas import tpu as pltpu
from jax.sharding import PartitionSpec as P

EMPTY = 2.0**22
VMEM_LIMIT = 40 * 1024 * 1024
LANES = 128
CHUNKS = 4
PACK_COST, SCORE_COSTS = 3 * 10**10, (10**10, 3 * 10**10, 1, 3 * 10**10)
HALVED = 2
TAIL = 16


def _nt(a, b):
    return lax.dot_general(a, b, (((1,), (1,)), ((), ())), preferred_element_type=jnp.float32)


def _as_bf16(mask):
    return mask.astype(jnp.float32).astype(jnp.bfloat16)


def _spans(slots):
    return -(-slots // LANES)


def _write_block(out, pick, unit, high, low, slots):
    block = jnp.dot(pick, unit, preferred_element_type=jnp.float32).astype(jnp.bfloat16)
    pieces = block.shape[1] // LANES
    for k in range(pieces):
        out[k * slots : (k + 1) * slots, :] = block[:, k * LANES : (k + 1) * LANES]
    spans = _spans(slots)
    lines = [part[:, i * LANES : (i + 1) * LANES] for part in (high, low) for i in range(spans)]
    lines.append(jnp.zeros((TAIL - 2 * spans, LANES), jnp.float32))
    out[pieces * slots :, :] = jnp.concatenate(lines, axis=0).astype(jnp.bfloat16)


def _block(parts, slots):
    pieces = [ref[k * slots : (k + 1) * slots, :] for ref in parts for k in range(ref.shape[0] // slots)]
    return jnp.concatenate(pieces, axis=1)


def _ranks(parts, slots):
    ref = parts[-1]
    tail = ref[ref.shape[0] - TAIL :, :].astype(jnp.float32)
    spans = _spans(slots)
    value = tail[:spans] * 256.0 + tail[spans : 2 * spans]
    return jnp.concatenate([value[i : i + 1] for i in range(spans)], axis=1)


def _pick(lab, pos, dest, low, high):
    key = jnp.where(lab == dest, pos, -1)
    return _as_bf16(lax.broadcasted_iota(jnp.int32, (high - low, lab.shape[1]), 0) + low == key)


def _pack_first(pieces, groups, slots, me_ref, emb_hbm, lab_hbm, prio_hbm, *rest):
    unit_ref, pos_ref, ranks_ref, *outs = rest[:-5]
    emb_ref, lab_ref, prio_ref, sems, word_sems = rest[-5:]
    rows = emb_ref.shape[0]
    words = [
        pltpu.make_async_copy(lab_hbm, lab_ref, word_sems.at[0]),
        pltpu.make_async_copy(prio_hbm, prio_ref, word_sems.at[1]),
    ]
    chunk = rows // CHUNKS
    spans = [pl.ds(i * chunk, chunk) for i in range(CHUNKS)]
    copies = [pltpu.make_async_copy(emb_hbm.at[span], emb_ref.at[span], sems.at[i]) for i, span in enumerate(spans)]
    for copy in words + copies:
        copy.start()
    for copy in words:
        copy.wait()
    lab = lab_ref[...]
    away = jnp.bitwise_xor(lax.broadcasted_iota(jnp.int32, (groups, rows), 0), me_ref[0])
    onehot = (away == lab).astype(jnp.float32)
    before = lax.broadcasted_iota(jnp.int32, (rows, rows), 0) < lax.broadcasted_iota(jnp.int32, (rows, rows), 1)
    earlier = jnp.dot(onehot.astype(jnp.bfloat16), _as_bf16(before), preferred_element_type=jnp.float32)
    pos = jnp.sum(onehot * earlier, axis=0, keepdims=True).astype(jnp.int32)
    pos_ref[...] = pos
    prio = jnp.concatenate([prio_ref[i : i + 1, :] for i in range(rows // LANES)], axis=1)
    high = (prio >> 8).astype(jnp.float32)
    low = (prio & 255).astype(jnp.float32)
    parts = jnp.concatenate([onehot * high, onehot * low, onehot], axis=0).astype(jnp.bfloat16)
    places = lax.broadcasted_iota(jnp.int32, (_spans(slots) * LANES, rows), 0)
    placed = _nt(parts, _as_bf16(places == pos))
    high = jnp.where(placed[2 * groups :] > 0.5, placed[:groups], EMPTY)
    low = placed[groups : 2 * groups]
    ranks_ref[...] = jnp.concatenate([high, low], axis=0)
    for copy, span in zip(copies, spans):
        copy.wait()
        emb = emb_ref[span, :].astype(jnp.float32)
        scale = lax.rsqrt(jnp.sum(emb * emb, axis=1, keepdims=True) + 1e-06)
        unit_ref[span, :] = (emb * scale).astype(jnp.bfloat16)
    unit = unit_ref[...]
    for (r, first, last), out in zip(pieces, outs):
        pick = _pick(lab, pos, jnp.bitwise_xor(me_ref[0], r), first, last)
        _write_block(out, pick, unit, high[r : r + 1, first:], low[r : r + 1, first:], last - first)


def _pack_rest(pieces, groups, me_ref, unit_ref, lab_ref, pos_ref, ranks_ref, *outs):
    for (r, first, last), out in zip(pieces, outs):
        pick = _pick(lab_ref[...], pos_ref[...], jnp.bitwise_xor(me_ref[0], r), first, last)
        high = ranks_ref[r : r + 1, first:]
        low = ranks_ref[groups + r : groups + r + 1, first:]
        _write_block(out, pick, unit_ref[...], high, low, last - first)


def _score(pieces, jobs, n_sib, n_old, final, me_ref, prev_ref, *rest):
    n = len(pieces)
    out_ref, rest = rest[-1], list(rest[:-1])
    sib_pieces = pieces[n - n_sib :] if final else pieces[:n_sib]
    sizes = [last - first for _, first, last in list(pieces) + list(sib_pieces)]
    blocks = []
    while rest:
        parts = [rest.pop(0)]
        whole = parts[0].shape[0] % sizes[len(blocks)] == TAIL
        blocks.append(parts if whole else parts + [rest.pop(0)])
    ranks = [_ranks(parts, size) for parts, size in zip(blocks, sizes)]
    lanes = max(rank.shape[1] for rank in ranks)
    padded = [jnp.concatenate([rank] * (lanes // rank.shape[1]), axis=1) for rank in ranks]
    columns = jnp.transpose(jnp.concatenate(padded, axis=0))

    rows = [None] * n
    for j in range(n_old):
        r, first, last = pieces[j]
        rows[j] = prev_ref[r : r + 1, first:last]
    for keys, queries in jobs:
        sim = _nt(
            jnp.concatenate([_block(blocks[i], sizes[i]) for i in keys], axis=0),
            jnp.concatenate([_block(blocks[j], sizes[j]) for j in queries], axis=0),
        )
        key_ranks = jnp.concatenate([columns[: sizes[i], i : i + 1] for i in keys], axis=0)
        query_ranks = jnp.concatenate([ranks[j][:, : sizes[j]] for j in queries], axis=1)
        best = jnp.max(jnp.where(key_ranks < query_ranks, sim, -1.0), axis=0, keepdims=True)
        start = 0
        for j in queries:
            row = best[:, start : start + sizes[j]]
            rows[j] = row if rows[j] is None else jnp.maximum(rows[j], row)
            start += sizes[j]
    if not final:
        for (r, first, last), row in zip(pieces, rows):
            out_ref[r : r + 1, first:last] = row
    else:
        for r in range(out_ref.shape[0]):
            whole = [row for piece, row in sorted(zip(pieces, rows), key=lambda pair: pair[0]) if piece[0] == r]
            out_ref[pl.ds(jnp.bitwise_xor(me_ref[0], r), 1), :] = jnp.concatenate(whole, axis=1)


def _select(groups, lab_ref, pos_ref, got_ref, out_ref):
    slots = got_ref.shape[1]
    rows = lab_ref.shape[1]
    got = got_ref[...]
    a = got.astype(jnp.bfloat16)
    rest = got - a.astype(jnp.float32)
    b = rest.astype(jnp.bfloat16)
    c = (rest - b.astype(jnp.float32)).astype(jnp.bfloat16)
    pick = _as_bf16(lax.broadcasted_iota(jnp.int32, (slots, rows), 0) == pos_ref[...])
    value = jnp.dot(a, pick, preferred_element_type=jnp.float32)
    value += jnp.dot(b, pick, preferred_element_type=jnp.float32)
    value += jnp.dot(c, pick, preferred_element_type=jnp.float32)
    mine = lax.broadcasted_iota(jnp.int32, (groups, rows), 0) == lab_ref[...]
    out_ref[...] = jnp.sum(jnp.where(mine, value, 0.0), axis=0)


SMEM = pl.BlockSpec(memory_space=pltpu.SMEM)
VMEM = pl.BlockSpec(memory_space=pltpu.VMEM)
HBM = pl.BlockSpec(memory_space=pltpu.HBM)


def local(embeddings, labels, priority):
    rows, width = embeddings.shape
    groups = lax.axis_size("wide")
    slots = 2 * rows // groups
    half = groups // 2
    me = lax.axis_index("wide").astype(jnp.int32).reshape(1)
    lab = labels.reshape(1, rows)

    def block(piece):
        return jax.ShapeDtypeStruct((width // LANES * (piece[2] - piece[1]) + TAIL, LANES), jnp.bfloat16)

    quarter = max(1, half // 4)
    near = [(r, 0, slots) for r in range(half)]
    far = [(r, 0, slots) for r in range(half, groups)]
    params = pltpu.CompilerParams(vmem_limit_bytes=VMEM_LIMIT)

    def in_hbm(x):
        return pltpu.with_memory_space_constraint(x, pltpu.HBM)

    unit, pos, ranks, *far_blocks = pl.pallas_call(
        functools.partial(_pack_first, far[:quarter], groups, slots),
        out_shape=[
            jax.ShapeDtypeStruct((rows, width), jnp.bfloat16),
            jax.ShapeDtypeStruct((1, rows), jnp.int32),
            jax.ShapeDtypeStruct((2 * groups, _spans(slots) * LANES), jnp.float32),
        ]
        + [block(piece) for piece in far[:quarter]],
        in_specs=[SMEM, HBM, HBM, HBM],
        out_specs=[VMEM] * (3 + quarter),
        scratch_shapes=[
            pltpu.VMEM((rows, width), jnp.bfloat16),
            pltpu.VMEM((1, rows), jnp.int32),
            pltpu.VMEM((rows // LANES, LANES), jnp.int32),
            pltpu.SemaphoreType.DMA((CHUNKS,)),
            pltpu.SemaphoreType.DMA((2,)),
        ],
        compiler_params=params,
        name="pack_first",
    )(me, in_hbm(embeddings), in_hbm(lab), in_hbm(priority.reshape(rows // LANES, LANES)))

    def swap(x):
        return lax.ppermute(x, "narrow", [(0, 1), (1, 0)])

    def send(x, r):
        return lax.ppermute(x, "wide", [(s, s ^ r) for s in range(groups)])

    def after(x, *others):
        return lax.optimization_barrier((x, *others))[0]

    def pack_rest(pieces, name):
        return pl.pallas_call(
            functools.partial(_pack_rest, pieces, groups),
            out_shape=[block(piece) for piece in pieces],
            in_specs=[SMEM] + [VMEM] * 4,
            out_specs=[VMEM] * len(pieces),
            compiler_params=params,
            cost_estimate=pl.CostEstimate(flops=PACK_COST, bytes_accessed=1, transcendentals=0),
            name=name,
        )(me, unit, lab, pos, ranks)

    far_blocks += pack_rest(far[quarter:], "pack_far")
    near_blocks = pack_rest(near, "pack_near")
    own = {}
    for i, piece in enumerate(far):
        out = far_blocks[i]
        if i >= 2 * quarter:
            out = after(out, own[far[i - 2 * quarter]])
        own[piece] = send(out, piece[0])
    for piece, out in zip(near, near_blocks):
        own[piece] = send(out, piece[0]) if piece[0] else out

    steps = [
        near[:1] + far[:quarter],
        far[quarter : 2 * quarter] + near[1:],
        far[2 * quarter : 3 * quarter],
        far[3 * quarter :],
    ]

    def score(pieces, partners, jobs, n_old, best, name, number, final=False):
        others = [part for piece in partners for part in sib[piece]]
        return pl.pallas_call(
            functools.partial(_score, pieces, jobs, len(partners), n_old, final),
            out_shape=jax.ShapeDtypeStruct((groups, slots), jnp.float32),
            in_specs=[SMEM] + [VMEM] * (1 + len(pieces) + len(others)),
            out_specs=VMEM,
            compiler_params=params,
            cost_estimate=pl.CostEstimate(flops=SCORE_COSTS[number], bytes_accessed=1, transcendentals=0),
            name=name,
        )(me, best, *[own[piece] for piece in pieces], *others)

    order, best, sib = [], jnp.zeros((groups, slots), jnp.float32), {}
    for number, step in enumerate(steps):
        for piece in step:
            ready = after(own[piece], best) if number >= HALVED else own[piece]
            cut = width // LANES // 2 * (piece[2] - piece[1])
            sib[piece] = [swap(part) for part in ((ready[:cut], ready[cut:]) if number == HALVED else (ready,))]
        n_old = len(order)
        order = order + step
        n = len(order)
        old, new = list(range(n_old)), list(range(n_old, n))
        if number < len(steps) - 1:
            jobs = [(new + [n + j for j in new], old)] if old else []
            best = score(order, order, jobs + [(list(range(2 * n)), new)], n_old, best, f"score_{number}", number)
        else:
            jobs = [(list(range(n + n_old)), new)]
            best = score(order, order[:n_old], jobs, n_old, best, f"score_{number}", number)
            jobs = [(new + list(range(n, 2 * n - n_old)), old + new)]
            best = score(order, step, jobs, n, best, "score_final", number, final=True)

    returned = lax.all_to_all(best, "wide", split_axis=0, concat_axis=0, tiled=True)
    return pl.pallas_call(
        functools.partial(_select, groups),
        out_shape=jax.ShapeDtypeStruct((rows,), jnp.float32),
        in_specs=[VMEM, VMEM, VMEM],
        out_specs=VMEM,
        compiler_params=params,
        name="select",
    )(lab, pos, returned)


def solution(mesh):
    in_specs = (
        P(("parts", "wide", "narrow"), None),
        P(("parts", "wide", "narrow"), None),
        P(("parts", "wide", "narrow")),
    )
    out_specs = P(("parts", "wide", "narrow"))
    return jax.shard_map(local, mesh=mesh, in_specs=in_specs, out_specs=out_specs, check_vma=False)
```

```python
import functools

import jax
import jax.numpy as jnp
from jax import lax
from jax.experimental import pallas as pl
from jax.experimental.pallas import tpu as pltpu
from jax.sharding import PartitionSpec as P

EMPTY = 2.0**22
VMEM_LIMIT = 40 * 1024 * 1024
LANES = 128
CHUNKS = 1
PACK_COST, SCORE_COSTS = 3 * 10**10, (10**10, 3 * 10**10, 1, 3 * 10**10)
HALVED = 2
TAIL = 16


def _nt(a, b):
    return lax.dot_general(a, b, (((1,), (1,)), ((), ())), preferred_element_type=jnp.float32)


def _as_bf16(mask):
    return mask.astype(jnp.float32).astype(jnp.bfloat16)


def _spans(slots):
    return -(-slots // LANES)


def _write_block(out, block, high, low, slots):
    scale = lax.rsqrt(jnp.sum(block * block, axis=1, keepdims=True) + 1e-06)
    block = (block * scale).astype(jnp.bfloat16)
    pieces = block.shape[1] // LANES
    for k in range(pieces):
        out[k * slots : (k + 1) * slots, :] = block[:, k * LANES : (k + 1) * LANES]
    spans = _spans(slots)
    lines = [part[:, i * LANES : (i + 1) * LANES] for part in (high, low) for i in range(spans)]
    lines.append(jnp.zeros((TAIL - 2 * spans, LANES), jnp.float32))
    out[pieces * slots :, :] = jnp.concatenate(lines, axis=0).astype(jnp.bfloat16)


def _block(parts, slots):
    pieces = [ref[k * slots : (k + 1) * slots, :] for ref in parts for k in range(ref.shape[0] // slots)]
    return jnp.concatenate(pieces, axis=1)


def _ranks(parts, slots):
    ref = parts[-1]
    tail = ref[ref.shape[0] - TAIL :, :].astype(jnp.float32)
    spans = _spans(slots)
    value = tail[:spans] * 256.0 + tail[spans : 2 * spans]
    return jnp.concatenate([value[i : i + 1] for i in range(spans)], axis=1)


def _pick(lab, pos, dest, low, high):
    key = jnp.where(lab == dest, pos, -1)
    return _as_bf16(lax.broadcasted_iota(jnp.int32, (high - low, lab.shape[1]), 0) + low == key)


def _pack_first(pieces, groups, slots, me_ref, emb_hbm, lab_hbm, prio_hbm, *rest):
    pos_ref, ranks_ref, *outs = rest[:-5]
    emb_ref, lab_ref, prio_ref, sems, word_sems = rest[-5:]
    rows = emb_ref.shape[0]
    words = [
        pltpu.make_async_copy(lab_hbm, lab_ref, word_sems.at[0]),
        pltpu.make_async_copy(prio_hbm, prio_ref, word_sems.at[1]),
    ]
    chunk = rows // CHUNKS
    spans = [pl.ds(i * chunk, chunk) for i in range(CHUNKS)]
    copies = [pltpu.make_async_copy(emb_hbm.at[span], emb_ref.at[span], sems.at[i]) for i, span in enumerate(spans)]
    for copy in words + copies:
        copy.start()
    earlier_rows = lax.broadcasted_iota(jnp.int32, (rows, rows), 0)
    before = _as_bf16(earlier_rows < lax.broadcasted_iota(jnp.int32, (rows, rows), 1))
    for copy in words:
        copy.wait()
    lab = lab_ref[...]
    away = jnp.bitwise_xor(lax.broadcasted_iota(jnp.int32, (groups, rows), 0), me_ref[0])
    onehot = (away == lab).astype(jnp.float32)
    earlier = jnp.dot(onehot.astype(jnp.bfloat16), before, preferred_element_type=jnp.float32)
    pos = jnp.sum(onehot * earlier, axis=0, keepdims=True).astype(jnp.int32)
    pos_ref[...] = pos
    prio = jnp.concatenate([prio_ref[i : i + 1, :] for i in range(rows // LANES)], axis=1)
    high = (prio >> 8).astype(jnp.float32)
    low = (prio & 255).astype(jnp.float32)
    parts = jnp.concatenate([onehot * high, onehot * low, onehot], axis=0).astype(jnp.bfloat16)
    places = lax.broadcasted_iota(jnp.int32, (_spans(slots) * LANES, rows), 0)
    placed = _nt(parts, _as_bf16(places == pos))
    high = jnp.where(placed[2 * groups :] > 0.5, placed[:groups], EMPTY)
    low = placed[groups : 2 * groups]
    ranks_ref[...] = jnp.concatenate([high, low], axis=0)
    picks = [_pick(lab, pos, jnp.bitwise_xor(me_ref[0], r), first, last) for r, first, last in pieces]
    sums = [0.0] * len(pieces)
    for i, copy in enumerate(copies):
        copy.wait()
        part = emb_ref[spans[i], :]
        for j, pick in enumerate(picks):
            sums[j] += jnp.dot(pick[:, i * chunk : (i + 1) * chunk], part, preferred_element_type=jnp.float32)
    for (r, first, last), out, block in zip(pieces, outs, sums):
        _write_block(out, block, high[r : r + 1, first:], low[r : r + 1, first:], last - first)


def _pack_rest(pieces, groups, me_ref, emb_ref, lab_ref, pos_ref, ranks_ref, *outs):
    for (r, first, last), out in zip(pieces, outs):
        pick = _pick(lab_ref[...], pos_ref[...], jnp.bitwise_xor(me_ref[0], r), first, last)
        high = ranks_ref[r : r + 1, first:]
        low = ranks_ref[groups + r : groups + r + 1, first:]
        block = jnp.dot(pick, emb_ref[...], preferred_element_type=jnp.float32)
        _write_block(out, block, high, low, last - first)


def _score(pieces, jobs, n_sib, n_old, final, me_ref, prev_ref, *rest):
    n = len(pieces)
    out_ref, rest = rest[-1], list(rest[:-1])
    sib_pieces = pieces[n - n_sib :] if final else pieces[:n_sib]
    sizes = [last - first for _, first, last in list(pieces) + list(sib_pieces)]
    blocks = []
    while rest:
        parts = [rest.pop(0)]
        whole = parts[0].shape[0] % sizes[len(blocks)] == TAIL
        blocks.append(parts if whole else parts + [rest.pop(0)])
    ranks = [_ranks(parts, size) for parts, size in zip(blocks, sizes)]
    lanes = max(rank.shape[1] for rank in ranks)
    padded = [jnp.concatenate([rank] * (lanes // rank.shape[1]), axis=1) for rank in ranks]
    columns = jnp.transpose(jnp.concatenate(padded, axis=0))

    rows = [None] * n
    for j in range(n_old):
        r, first, last = pieces[j]
        rows[j] = prev_ref[r : r + 1, first:last]
    for keys, queries in jobs:
        sim = _nt(
            jnp.concatenate([_block(blocks[i], sizes[i]) for i in keys], axis=0),
            jnp.concatenate([_block(blocks[j], sizes[j]) for j in queries], axis=0),
        )
        key_ranks = jnp.concatenate([columns[: sizes[i], i : i + 1] for i in keys], axis=0)
        query_ranks = jnp.concatenate([ranks[j][:, : sizes[j]] for j in queries], axis=1)
        best = jnp.max(jnp.where(key_ranks < query_ranks, sim, -1.0), axis=0, keepdims=True)
        start = 0
        for j in queries:
            row = best[:, start : start + sizes[j]]
            rows[j] = row if rows[j] is None else jnp.maximum(rows[j], row)
            start += sizes[j]
    if not final:
        for (r, first, last), row in zip(pieces, rows):
            out_ref[r : r + 1, first:last] = row
    else:
        for r in range(out_ref.shape[0]):
            whole = [row for piece, row in sorted(zip(pieces, rows), key=lambda pair: pair[0]) if piece[0] == r]
            out_ref[pl.ds(jnp.bitwise_xor(me_ref[0], r), 1), :] = jnp.concatenate(whole, axis=1)


def _select(groups, lab_ref, pos_ref, got_ref, out_ref):
    slots = got_ref.shape[1]
    rows = lab_ref.shape[1]
    got = got_ref[...]
    a = got.astype(jnp.bfloat16)
    rest = got - a.astype(jnp.float32)
    b = rest.astype(jnp.bfloat16)
    c = (rest - b.astype(jnp.float32)).astype(jnp.bfloat16)
    pick = _as_bf16(lax.broadcasted_iota(jnp.int32, (slots, rows), 0) == pos_ref[...])
    value = jnp.dot(a, pick, preferred_element_type=jnp.float32)
    value += jnp.dot(b, pick, preferred_element_type=jnp.float32)
    value += jnp.dot(c, pick, preferred_element_type=jnp.float32)
    mine = lax.broadcasted_iota(jnp.int32, (groups, rows), 0) == lab_ref[...]
    out_ref[...] = jnp.sum(jnp.where(mine, value, 0.0), axis=0)


SMEM = pl.BlockSpec(memory_space=pltpu.SMEM)
VMEM = pl.BlockSpec(memory_space=pltpu.VMEM)
HBM = pl.BlockSpec(memory_space=pltpu.HBM)


def local(embeddings, labels, priority):
    rows, width = embeddings.shape
    groups = lax.axis_size("wide")
    slots = 2 * rows // groups
    half = groups // 2
    me = lax.axis_index("wide").astype(jnp.int32).reshape(1)
    lab = labels.reshape(1, rows)

    def block(piece):
        return jax.ShapeDtypeStruct((width // LANES * (piece[2] - piece[1]) + TAIL, LANES), jnp.bfloat16)

    quarter = max(1, half // 4)
    near = [(r, 0, slots) for r in range(half)]
    far = [(r, 0, slots) for r in range(half, groups)]
    params = pltpu.CompilerParams(vmem_limit_bytes=VMEM_LIMIT)

    def in_hbm(x):
        return pltpu.with_memory_space_constraint(x, pltpu.HBM)

    pos, ranks, *far_blocks = pl.pallas_call(
        functools.partial(_pack_first, far[:quarter], groups, slots),
        out_shape=[
            jax.ShapeDtypeStruct((1, rows), jnp.int32),
            jax.ShapeDtypeStruct((2 * groups, _spans(slots) * LANES), jnp.float32),
        ]
        + [block(piece) for piece in far[:quarter]],
        in_specs=[SMEM, HBM, HBM, HBM],
        out_specs=[VMEM] * (2 + quarter),
        scratch_shapes=[
            pltpu.VMEM((rows, width), jnp.bfloat16),
            pltpu.VMEM((1, rows), jnp.int32),
            pltpu.VMEM((rows // LANES, LANES), jnp.int32),
            pltpu.SemaphoreType.DMA((CHUNKS,)),
            pltpu.SemaphoreType.DMA((2,)),
        ],
        compiler_params=params,
        name="pack_first",
    )(me, in_hbm(embeddings), in_hbm(lab), in_hbm(priority.reshape(rows // LANES, LANES)))

    def swap(x):
        return lax.ppermute(x, "narrow", [(0, 1), (1, 0)])

    def send(x, r):
        return lax.ppermute(x, "wide", [(s, s ^ r) for s in range(groups)])

    def after(x, *others):
        return lax.optimization_barrier((x, *others))[0]

    def pack_rest(pieces, name):
        return pl.pallas_call(
            functools.partial(_pack_rest, pieces, groups),
            out_shape=[block(piece) for piece in pieces],
            in_specs=[SMEM] + [VMEM] * 4,
            out_specs=[VMEM] * len(pieces),
            compiler_params=params,
            cost_estimate=pl.CostEstimate(flops=PACK_COST, bytes_accessed=1, transcendentals=0),
            name=name,
        )(me, embeddings, lab, pos, ranks)

    far_blocks += pack_rest(far[quarter:], "pack_far")
    near_blocks = pack_rest(near, "pack_near")
    own = {}
    for i, piece in enumerate(far):
        out = far_blocks[i]
        if i >= 2 * quarter:
            out = after(out, own[far[i - 2 * quarter]])
        own[piece] = send(out, piece[0])
    for piece, out in zip(near, near_blocks):
        own[piece] = send(out, piece[0]) if piece[0] else out

    steps = [
        near[:1] + far[:quarter],
        far[quarter : 2 * quarter] + near[1:],
        far[2 * quarter : 3 * quarter],
        far[3 * quarter :],
    ]

    def score(pieces, partners, jobs, n_old, best, name, number, final=False):
        others = [part for piece in partners for part in sib[piece]]
        return pl.pallas_call(
            functools.partial(_score, pieces, jobs, len(partners), n_old, final),
            out_shape=jax.ShapeDtypeStruct((groups, slots), jnp.float32),
            in_specs=[SMEM] + [VMEM] * (1 + len(pieces) + len(others)),
            out_specs=VMEM,
            compiler_params=params,
            cost_estimate=pl.CostEstimate(flops=SCORE_COSTS[number], bytes_accessed=1, transcendentals=0),
            name=name,
        )(me, best, *[own[piece] for piece in pieces], *others)

    order, best, sib = [], jnp.zeros((groups, slots), jnp.float32), {}
    for number, step in enumerate(steps):
        for piece in step:
            ready = after(own[piece], best) if number >= HALVED else own[piece]
            cut = width // LANES // 2 * (piece[2] - piece[1])
            sib[piece] = [swap(part) for part in ((ready[:cut], ready[cut:]) if number == HALVED else (ready,))]
        n_old = len(order)
        order = order + step
        n = len(order)
        old, new = list(range(n_old)), list(range(n_old, n))
        if number < len(steps) - 1:
            jobs = [(new + [n + j for j in new], old)] if old else []
            best = score(order, order, jobs + [(list(range(2 * n)), new)], n_old, best, f"score_{number}", number)
        else:
            jobs = [(list(range(n + n_old)), new)]
            best = score(order, order[:n_old], jobs, n_old, best, f"score_{number}", number)
            jobs = [(new + list(range(n, 2 * n - n_old)), old + new)]
            best = score(order, step, jobs, n, best, "score_final", number, final=True)

    returned = lax.all_to_all(best, "wide", split_axis=0, concat_axis=0, tiled=True)
    return pl.pallas_call(
        functools.partial(_select, groups),
        out_shape=jax.ShapeDtypeStruct((rows,), jnp.float32),
        in_specs=[VMEM, VMEM, VMEM],
        out_specs=VMEM,
        compiler_params=params,
        name="select",
    )(lab, pos, returned)


def solution(mesh):
    in_specs = (
        P(("parts", "wide", "narrow"), None),
        P(("parts", "wide", "narrow"), None),
        P(("parts", "wide", "narrow")),
    )
    out_specs = P(("parts", "wide", "narrow"))
    return jax.shard_map(local, mesh=mesh, in_specs=in_specs, out_specs=out_specs, check_vma=False)
```

```python
import functools

import jax
import jax.numpy as jnp
from jax import lax
from jax.experimental import pallas as pl
from jax.experimental.pallas import tpu as pltpu
from jax.sharding import PartitionSpec as P

EMPTY = 2.0**22
VMEM_LIMIT = 40 * 1024 * 1024
LANES = 128
CHUNKS = 1
PACK_COST, SCORE_COSTS = 3 * 10**10, (10**10, 3 * 10**10, 1, 3 * 10**10)
HALVED = 2
TAIL = 16


def _nt(a, b):
    return lax.dot_general(a, b, (((1,), (1,)), ((), ())), preferred_element_type=jnp.float32)


def _as_bf16(mask):
    return mask.astype(jnp.float32).astype(jnp.bfloat16)


def _spans(slots):
    return -(-slots // LANES)


def _write_block(out, block, high, low, slots):
    scale = lax.rsqrt(jnp.sum(block * block, axis=1, keepdims=True) + 1e-06)
    block = (block * scale).astype(jnp.bfloat16)
    pieces = block.shape[1] // LANES
    for k in range(pieces):
        out[k * slots : (k + 1) * slots, :] = block[:, k * LANES : (k + 1) * LANES]
    spans = _spans(slots)
    lines = [part[:, i * LANES : (i + 1) * LANES] for part in (high, low) for i in range(spans)]
    lines.append(jnp.zeros((TAIL - 2 * spans, LANES), jnp.float32))
    out[pieces * slots :, :] = jnp.concatenate(lines, axis=0).astype(jnp.bfloat16)


def _block(parts, slots):
    pieces = [ref[k * slots : (k + 1) * slots, :] for ref in parts for k in range(ref.shape[0] // slots)]
    return jnp.concatenate(pieces, axis=1)


def _ranks(parts, slots):
    ref = parts[-1]
    tail = ref[ref.shape[0] - TAIL :, :].astype(jnp.float32)
    spans = _spans(slots)
    value = tail[:spans] * 256.0 + tail[spans : 2 * spans]
    return jnp.concatenate([value[i : i + 1] for i in range(spans)], axis=1)


def _pick(lab, pos, dest, low, high):
    key = jnp.where(lab == dest, pos, -1)
    return _as_bf16(lax.broadcasted_iota(jnp.int32, (high - low, lab.shape[1]), 0) + low == key)


def _pack_first(pieces, groups, slots, me_ref, emb_hbm, lab_hbm, prio_hbm, *rest):
    pos_ref, ranks_ref, *outs = rest[:-5]
    emb_ref, lab_ref, prio_ref, sems, word_sems = rest[-5:]
    rows = emb_ref.shape[0]
    words = [
        pltpu.make_async_copy(lab_hbm, lab_ref, word_sems.at[0]),
        pltpu.make_async_copy(prio_hbm, prio_ref, word_sems.at[1]),
    ]
    chunk = rows // CHUNKS
    spans = [pl.ds(i * chunk, chunk) for i in range(CHUNKS)]
    copies = [pltpu.make_async_copy(emb_hbm.at[span], emb_ref.at[span], sems.at[i]) for i, span in enumerate(spans)]
    for copy in words + copies:
        copy.start()
    earlier_rows = lax.broadcasted_iota(jnp.int32, (rows, rows), 0)
    before = _as_bf16(earlier_rows < lax.broadcasted_iota(jnp.int32, (rows, rows), 1))
    for copy in words:
        copy.wait()
    lab = lab_ref[...]
    away = jnp.bitwise_xor(lax.broadcasted_iota(jnp.int32, (groups, rows), 0), me_ref[0])
    onehot = (away == lab).astype(jnp.float32)
    earlier = jnp.dot(onehot.astype(jnp.bfloat16), before, preferred_element_type=jnp.float32)
    pos = jnp.sum(onehot * earlier, axis=0, keepdims=True).astype(jnp.int32)
    pos_ref[...] = pos
    prio = jnp.concatenate([prio_ref[i : i + 1, :] for i in range(rows // LANES)], axis=1)
    high = (prio >> 8).astype(jnp.float32)
    low = (prio & 255).astype(jnp.float32)
    parts = jnp.concatenate([onehot * high, onehot * low, onehot], axis=0).astype(jnp.bfloat16)
    places = lax.broadcasted_iota(jnp.int32, (_spans(slots) * LANES, rows), 0)
    placed = _nt(parts, _as_bf16(places == pos))
    high = jnp.where(placed[2 * groups :] > 0.5, placed[:groups], EMPTY)
    low = placed[groups : 2 * groups]
    ranks_ref[...] = jnp.concatenate([high, low], axis=0)
    picks = [_pick(lab, pos, jnp.bitwise_xor(me_ref[0], r), first, last) for r, first, last in pieces]
    sums = [0.0] * len(pieces)
    for i, copy in enumerate(copies):
        copy.wait()
        part = emb_ref[spans[i], :]
        for j, pick in enumerate(picks):
            sums[j] += jnp.dot(pick[:, i * chunk : (i + 1) * chunk], part, preferred_element_type=jnp.float32)
    for (r, first, last), out, block in zip(pieces, outs, sums):
        _write_block(out, block, high[r : r + 1, first:], low[r : r + 1, first:], last - first)


def _pack_rest(pieces, groups, me_ref, emb_ref, lab_ref, pos_ref, ranks_ref, *outs):
    for (r, first, last), out in zip(pieces, outs):
        pick = _pick(lab_ref[...], pos_ref[...], jnp.bitwise_xor(me_ref[0], r), first, last)
        high = ranks_ref[r : r + 1, first:]
        low = ranks_ref[groups + r : groups + r + 1, first:]
        block = jnp.dot(pick, emb_ref[...], preferred_element_type=jnp.float32)
        _write_block(out, block, high, low, last - first)


def _score(pieces, jobs, n_sib, n_old, final, me_ref, prev_ref, *rest):
    n = len(pieces)
    out_ref, rest = rest[-1], list(rest[:-1])
    sib_pieces = pieces[n - n_sib :] if final else pieces[:n_sib]
    sizes = [last - first for _, first, last in list(pieces) + list(sib_pieces)]
    blocks = []
    while rest:
        parts = [rest.pop(0)]
        whole = parts[0].shape[0] % sizes[len(blocks)] == TAIL
        blocks.append(parts if whole else parts + [rest.pop(0)])
    ranks = [_ranks(parts, size) for parts, size in zip(blocks, sizes)]
    lanes = max(rank.shape[1] for rank in ranks)
    padded = [jnp.concatenate([rank] * (lanes // rank.shape[1]), axis=1) for rank in ranks]
    columns = jnp.transpose(jnp.concatenate(padded, axis=0))

    rows = [None] * n
    for j in range(n_old):
        r, first, last = pieces[j]
        rows[j] = prev_ref[r : r + 1, first:last]
    for keys, queries in jobs:
        sim = _nt(
            jnp.concatenate([_block(blocks[i], sizes[i]) for i in keys], axis=0),
            jnp.concatenate([_block(blocks[j], sizes[j]) for j in queries], axis=0),
        )
        key_ranks = jnp.concatenate([columns[: sizes[i], i : i + 1] for i in keys], axis=0)
        query_ranks = jnp.concatenate([ranks[j][:, : sizes[j]] for j in queries], axis=1)
        best = jnp.max(jnp.where(key_ranks < query_ranks, sim, -1.0), axis=0, keepdims=True)
        start = 0
        for j in queries:
            row = best[:, start : start + sizes[j]]
            rows[j] = row if rows[j] is None else jnp.maximum(rows[j], row)
            start += sizes[j]
    if not final:
        for (r, first, last), row in zip(pieces, rows):
            out_ref[r : r + 1, first:last] = row
    else:
        for r in range(out_ref.shape[0]):
            whole = [row for piece, row in sorted(zip(pieces, rows), key=lambda pair: pair[0]) if piece[0] == r]
            out_ref[pl.ds(jnp.bitwise_xor(me_ref[0], r), 1), :] = jnp.concatenate(whole, axis=1)


def _select(groups, lab_ref, pos_ref, got_ref, out_ref):
    slots = got_ref.shape[1]
    rows = lab_ref.shape[1]
    got = got_ref[...]
    a = got.astype(jnp.bfloat16)
    rest = got - a.astype(jnp.float32)
    b = rest.astype(jnp.bfloat16)
    c = (rest - b.astype(jnp.float32)).astype(jnp.bfloat16)
    pick = _as_bf16(lax.broadcasted_iota(jnp.int32, (slots, rows), 0) == pos_ref[...])
    value = jnp.dot(a, pick, preferred_element_type=jnp.float32)
    value += jnp.dot(b, pick, preferred_element_type=jnp.float32)
    value += jnp.dot(c, pick, preferred_element_type=jnp.float32)
    mine = lax.broadcasted_iota(jnp.int32, (groups, rows), 0) == lab_ref[...]
    out_ref[...] = jnp.sum(jnp.where(mine, value, 0.0), axis=0)


SMEM = pl.BlockSpec(memory_space=pltpu.SMEM)
VMEM = pl.BlockSpec(memory_space=pltpu.VMEM)
HBM = pl.BlockSpec(memory_space=pltpu.HBM)


def local(embeddings, labels, priority):
    rows, width = embeddings.shape
    groups = lax.axis_size("wide")
    slots = 2 * rows // groups
    half = groups // 2
    me = lax.axis_index("wide").astype(jnp.int32).reshape(1)
    lab = labels.reshape(1, rows)

    def block(piece):
        return jax.ShapeDtypeStruct((width // LANES * (piece[2] - piece[1]) + TAIL, LANES), jnp.bfloat16)

    quarter = max(1, half // 4)
    near = [(r, 0, slots) for r in range(half)]
    far = [(r, 0, slots) for r in range(half, groups)]
    params = pltpu.CompilerParams(vmem_limit_bytes=VMEM_LIMIT)

    def in_hbm(x):
        return pltpu.with_memory_space_constraint(x, pltpu.HBM)

    pos, ranks, *far_blocks = pl.pallas_call(
        functools.partial(_pack_first, far[:quarter], groups, slots),
        out_shape=[
            jax.ShapeDtypeStruct((1, rows), jnp.int32),
            jax.ShapeDtypeStruct((2 * groups, _spans(slots) * LANES), jnp.float32),
        ]
        + [block(piece) for piece in far[:quarter]],
        in_specs=[SMEM, HBM, HBM, HBM],
        out_specs=[VMEM] * (2 + quarter),
        scratch_shapes=[
            pltpu.VMEM((rows, width), jnp.bfloat16),
            pltpu.VMEM((1, rows), jnp.int32),
            pltpu.VMEM((rows // LANES, LANES), jnp.int32),
            pltpu.SemaphoreType.DMA((CHUNKS,)),
            pltpu.SemaphoreType.DMA((2,)),
        ],
        compiler_params=params,
        name="pack_first",
    )(me, in_hbm(embeddings), in_hbm(lab), in_hbm(priority.reshape(rows // LANES, LANES)))

    def swap(x):
        return lax.ppermute(x, "narrow", [(0, 1), (1, 0)])

    def send(x, r):
        return lax.ppermute(x, "wide", [(s, s ^ r) for s in range(groups)])

    def after(x, *others):
        return lax.optimization_barrier((x, *others))[0]

    def pack_rest(pieces, name):
        return pl.pallas_call(
            functools.partial(_pack_rest, pieces, groups),
            out_shape=[block(piece) for piece in pieces],
            in_specs=[SMEM] + [VMEM] * 4,
            out_specs=[VMEM] * len(pieces),
            compiler_params=params,
            cost_estimate=pl.CostEstimate(flops=PACK_COST, bytes_accessed=1, transcendentals=0),
            name=name,
        )(me, embeddings, lab, pos, ranks)

    later = pack_rest(far[quarter:] + near, "pack_rest")
    far_blocks += later[: -len(near)]
    near_blocks = later[-len(near) :]
    own = {}
    for i, piece in enumerate(far):
        out = far_blocks[i]
        if i >= 2 * quarter:
            out = after(out, own[far[i - 2 * quarter]])
        own[piece] = send(out, piece[0])
    for piece, out in zip(near, near_blocks):
        own[piece] = send(out, piece[0]) if piece[0] else out

    steps = [
        near[:1] + far[:quarter],
        far[quarter : 2 * quarter] + near[1:],
        far[2 * quarter : 3 * quarter],
        far[3 * quarter :],
    ]

    def score(pieces, partners, jobs, n_old, best, name, number, final=False):
        others = [part for piece in partners for part in sib[piece]]
        return pl.pallas_call(
            functools.partial(_score, pieces, jobs, len(partners), n_old, final),
            out_shape=jax.ShapeDtypeStruct((groups, slots), jnp.float32),
            in_specs=[SMEM] + [VMEM] * (1 + len(pieces) + len(others)),
            out_specs=VMEM,
            compiler_params=params,
            cost_estimate=pl.CostEstimate(flops=SCORE_COSTS[number], bytes_accessed=1, transcendentals=0),
            name=name,
        )(me, best, *[own[piece] for piece in pieces], *others)

    order, best, sib = [], jnp.zeros((groups, slots), jnp.float32), {}
    for number, step in enumerate(steps):
        for piece in step:
            ready = after(own[piece], best) if number >= HALVED else own[piece]
            cut = width // LANES // 2 * (piece[2] - piece[1])
            sib[piece] = [swap(part) for part in ((ready[:cut], ready[cut:]) if number == HALVED else (ready,))]
        n_old = len(order)
        order = order + step
        n = len(order)
        old, new = list(range(n_old)), list(range(n_old, n))
        if number < len(steps) - 1:
            jobs = [(new + [n + j for j in new], old)] if old else []
            best = score(order, order, jobs + [(list(range(2 * n)), new)], n_old, best, f"score_{number}", number)
        else:
            jobs = [(list(range(n + n_old)), new)]
            best = score(order, order[:n_old], jobs, n_old, best, f"score_{number}", number)
            jobs = [(new + list(range(n, 2 * n - n_old)), old + new)]
            best = score(order, step, jobs, n, best, "score_final", number, final=True)

    returned = lax.all_to_all(best, "wide", split_axis=0, concat_axis=0, tiled=True)
    return pl.pallas_call(
        functools.partial(_select, groups),
        out_shape=jax.ShapeDtypeStruct((rows,), jnp.float32),
        in_specs=[VMEM, VMEM, VMEM],
        out_specs=VMEM,
        compiler_params=params,
        name="select",
    )(lab, pos, returned)


def solution(mesh):
    in_specs = (
        P(("parts", "wide", "narrow"), None),
        P(("parts", "wide", "narrow"), None),
        P(("parts", "wide", "narrow")),
    )
    out_specs = P(("parts", "wide", "narrow"))
    return jax.shard_map(local, mesh=mesh, in_specs=in_specs, out_specs=out_specs, check_vma=False)
```

```python
import functools

import jax
import jax.numpy as jnp
from jax import lax
from jax.experimental import pallas as pl
from jax.experimental.pallas import tpu as pltpu
from jax.sharding import PartitionSpec as P

EMPTY = 2.0**22
VMEM_LIMIT = 40 * 1024 * 1024
LANES = 128
CHUNKS = 1
PACK_COST, SCORE_COSTS = 3 * 10**10, (10**10, 3 * 10**10, 1, 3 * 10**10)
HALVED = 2
TAIL = 16


def _nt(a, b):
    return lax.dot_general(a, b, (((1,), (1,)), ((), ())), preferred_element_type=jnp.float32)


def _as_bf16(mask):
    return mask.astype(jnp.float32).astype(jnp.bfloat16)


def _spans(slots):
    return -(-slots // LANES)


def _write_block(out, block, high, low, slots):
    scale = lax.rsqrt(jnp.sum(block * block, axis=1, keepdims=True) + 1e-06)
    block = (block * scale).astype(jnp.bfloat16)
    pieces = block.shape[1] // LANES
    for k in range(pieces):
        out[k * slots : (k + 1) * slots, :] = block[:, k * LANES : (k + 1) * LANES]
    spans = _spans(slots)
    lines = [part[:, i * LANES : (i + 1) * LANES] for part in (high, low) for i in range(spans)]
    lines.append(jnp.zeros((TAIL - 2 * spans, LANES), jnp.float32))
    out[pieces * slots :, :] = jnp.concatenate(lines, axis=0).astype(jnp.bfloat16)


def _block(parts, slots):
    pieces = [ref[k * slots : (k + 1) * slots, :] for ref in parts for k in range(ref.shape[0] // slots)]
    return jnp.concatenate(pieces, axis=1)


def _ranks(parts, slots):
    ref = parts[-1]
    tail = ref[ref.shape[0] - TAIL :, :].astype(jnp.float32)
    spans = _spans(slots)
    value = tail[:spans] * 256.0 + tail[spans : 2 * spans]
    return jnp.concatenate([value[i : i + 1] for i in range(spans)], axis=1)


def _pick(lab, pos, dest, low, high):
    key = jnp.where(lab == dest, pos, -1)
    return _as_bf16(lax.broadcasted_iota(jnp.int32, (high - low, lab.shape[1]), 0) + low == key)


def _pack_first(pieces, groups, slots, me_ref, emb_hbm, lab_hbm, prio_hbm, *rest):
    pos_ref, ranks_ref, *outs = rest[:-5]
    emb_ref, lab_ref, prio_ref, sems, word_sems = rest[-5:]
    rows = emb_ref.shape[0]
    words = [
        pltpu.make_async_copy(lab_hbm, lab_ref, word_sems.at[0]),
        pltpu.make_async_copy(prio_hbm, prio_ref, word_sems.at[1]),
    ]
    chunk = rows // CHUNKS
    spans = [pl.ds(i * chunk, chunk) for i in range(CHUNKS)]
    copies = [pltpu.make_async_copy(emb_hbm.at[span], emb_ref.at[span], sems.at[i]) for i, span in enumerate(spans)]
    for copy in words + copies:
        copy.start()
    earlier_rows = lax.broadcasted_iota(jnp.int32, (rows, rows), 0)
    before = _as_bf16(earlier_rows < lax.broadcasted_iota(jnp.int32, (rows, rows), 1))
    for copy in words:
        copy.wait()
    lab = lab_ref[...]
    away = jnp.bitwise_xor(lax.broadcasted_iota(jnp.int32, (groups, rows), 0), me_ref[0])
    onehot = (away == lab).astype(jnp.float32)
    earlier = jnp.dot(onehot.astype(jnp.bfloat16), before, preferred_element_type=jnp.float32)
    pos = jnp.sum(onehot * earlier, axis=0, keepdims=True).astype(jnp.int32)
    pos_ref[...] = pos
    prio = jnp.concatenate([prio_ref[i : i + 1, :] for i in range(rows // LANES)], axis=1)
    high = (prio >> 8).astype(jnp.float32)
    low = (prio & 255).astype(jnp.float32)
    parts = jnp.concatenate([onehot * high, onehot * low, onehot], axis=0).astype(jnp.bfloat16)
    places = lax.broadcasted_iota(jnp.int32, (_spans(slots) * LANES, rows), 0)
    placed = _nt(parts, _as_bf16(places == pos))
    high = jnp.where(placed[2 * groups :] > 0.5, placed[:groups], EMPTY)
    low = placed[groups : 2 * groups]
    ranks_ref[...] = jnp.concatenate([high, low], axis=0)
    picks = [_pick(lab, pos, jnp.bitwise_xor(me_ref[0], r), first, last) for r, first, last in pieces]
    sums = [0.0] * len(pieces)
    for i, copy in enumerate(copies):
        copy.wait()
        part = emb_ref[spans[i], :]
        for j, pick in enumerate(picks):
            sums[j] += jnp.dot(pick[:, i * chunk : (i + 1) * chunk], part, preferred_element_type=jnp.float32)
    for (r, first, last), out, block in zip(pieces, outs, sums):
        _write_block(out, block, high[r : r + 1, first:], low[r : r + 1, first:], last - first)


def _pack_rest(pieces, groups, me_ref, emb_ref, lab_ref, pos_ref, ranks_ref, *outs):
    for (r, first, last), out in zip(pieces, outs):
        pick = _pick(lab_ref[...], pos_ref[...], jnp.bitwise_xor(me_ref[0], r), first, last)
        high = ranks_ref[r : r + 1, first:]
        low = ranks_ref[groups + r : groups + r + 1, first:]
        block = jnp.dot(pick, emb_ref[...], preferred_element_type=jnp.float32)
        _write_block(out, block, high, low, last - first)


def _score(pieces, jobs, n_sib, n_old, final, me_ref, prev_ref, *rest):
    n = len(pieces)
    out_ref, rest = rest[-1], list(rest[:-1])
    sib_pieces = pieces[n - n_sib :] if final else pieces[:n_sib]
    sizes = [last - first for _, first, last in list(pieces) + list(sib_pieces)]
    blocks = []
    while rest:
        parts = [rest.pop(0)]
        whole = parts[0].shape[0] % sizes[len(blocks)] == TAIL
        blocks.append(parts if whole else parts + [rest.pop(0)])
    ranks = [_ranks(parts, size) for parts, size in zip(blocks, sizes)]
    lanes = max(rank.shape[1] for rank in ranks)
    padded = [jnp.concatenate([rank] * (lanes // rank.shape[1]), axis=1) for rank in ranks]
    columns = jnp.transpose(jnp.concatenate(padded, axis=0))

    rows = [None] * n
    for j in range(n_old):
        r, first, last = pieces[j]
        rows[j] = prev_ref[r : r + 1, first:last]
    for keys, queries in jobs:
        sim = _nt(
            jnp.concatenate([_block(blocks[i], sizes[i]) for i in keys], axis=0),
            jnp.concatenate([_block(blocks[j], sizes[j]) for j in queries], axis=0),
        )
        key_ranks = jnp.concatenate([columns[: sizes[i], i : i + 1] for i in keys], axis=0)
        query_ranks = jnp.concatenate([ranks[j][:, : sizes[j]] for j in queries], axis=1)
        best = jnp.max(jnp.where(key_ranks < query_ranks, sim, -1.0), axis=0, keepdims=True)
        start = 0
        for j in queries:
            row = best[:, start : start + sizes[j]]
            rows[j] = row if rows[j] is None else jnp.maximum(rows[j], row)
            start += sizes[j]
    if not final:
        for (r, first, last), row in zip(pieces, rows):
            out_ref[r : r + 1, first:last] = row
    else:
        for r in range(out_ref.shape[0]):
            whole = [row for piece, row in sorted(zip(pieces, rows), key=lambda pair: pair[0]) if piece[0] == r]
            out_ref[pl.ds(jnp.bitwise_xor(me_ref[0], r), 1), :] = jnp.concatenate(whole, axis=1)


def _select(groups, lab_ref, pos_ref, got_ref, out_ref):
    slots = got_ref.shape[1]
    rows = lab_ref.shape[1]
    got = got_ref[...]
    a = got.astype(jnp.bfloat16)
    rest = got - a.astype(jnp.float32)
    b = rest.astype(jnp.bfloat16)
    c = (rest - b.astype(jnp.float32)).astype(jnp.bfloat16)
    pick = _as_bf16(lax.broadcasted_iota(jnp.int32, (slots, rows), 0) == pos_ref[...])
    parts = jnp.dot(jnp.concatenate([a, b, c], axis=0), pick, preferred_element_type=jnp.float32)
    value = parts[:groups] + parts[groups : 2 * groups] + parts[2 * groups :]
    mine = lax.broadcasted_iota(jnp.int32, (groups, rows), 0) == lab_ref[...]
    out_ref[...] = jnp.sum(jnp.where(mine, value, 0.0), axis=0)


SMEM = pl.BlockSpec(memory_space=pltpu.SMEM)
VMEM = pl.BlockSpec(memory_space=pltpu.VMEM)
HBM = pl.BlockSpec(memory_space=pltpu.HBM)


def local(embeddings, labels, priority):
    rows, width = embeddings.shape
    groups = lax.axis_size("wide")
    slots = 2 * rows // groups
    half = groups // 2
    me = lax.axis_index("wide").astype(jnp.int32).reshape(1)
    lab = labels.reshape(1, rows)

    def block(piece):
        return jax.ShapeDtypeStruct((width // LANES * (piece[2] - piece[1]) + TAIL, LANES), jnp.bfloat16)

    quarter = max(1, half // 4)
    near = [(r, 0, slots) for r in range(half)]
    far = [(r, 0, slots) for r in range(half, groups)]
    params = pltpu.CompilerParams(vmem_limit_bytes=VMEM_LIMIT)

    def in_hbm(x):
        return pltpu.with_memory_space_constraint(x, pltpu.HBM)

    pos, ranks, *far_blocks = pl.pallas_call(
        functools.partial(_pack_first, far[:quarter], groups, slots),
        out_shape=[
            jax.ShapeDtypeStruct((1, rows), jnp.int32),
            jax.ShapeDtypeStruct((2 * groups, _spans(slots) * LANES), jnp.float32),
        ]
        + [block(piece) for piece in far[:quarter]],
        in_specs=[SMEM, HBM, HBM, HBM],
        out_specs=[VMEM] * (2 + quarter),
        scratch_shapes=[
            pltpu.VMEM((rows, width), jnp.bfloat16),
            pltpu.VMEM((1, rows), jnp.int32),
            pltpu.VMEM((rows // LANES, LANES), jnp.int32),
            pltpu.SemaphoreType.DMA((CHUNKS,)),
            pltpu.SemaphoreType.DMA((2,)),
        ],
        compiler_params=params,
        name="pack_first",
    )(me, in_hbm(embeddings), in_hbm(lab), in_hbm(priority.reshape(rows // LANES, LANES)))

    def swap(x):
        return lax.ppermute(x, "narrow", [(0, 1), (1, 0)])

    def send(x, r):
        return lax.ppermute(x, "wide", [(s, s ^ r) for s in range(groups)])

    def after(x, *others):
        return lax.optimization_barrier((x, *others))[0]

    def pack_rest(pieces, name):
        return pl.pallas_call(
            functools.partial(_pack_rest, pieces, groups),
            out_shape=[block(piece) for piece in pieces],
            in_specs=[SMEM] + [VMEM] * 4,
            out_specs=[VMEM] * len(pieces),
            compiler_params=params,
            cost_estimate=pl.CostEstimate(flops=PACK_COST, bytes_accessed=1, transcendentals=0),
            name=name,
        )(me, embeddings, lab, pos, ranks)

    later = pack_rest(far[quarter:] + near, "pack_rest")
    far_blocks += later[: -len(near)]
    near_blocks = later[-len(near) :]
    own = {}
    for i, piece in enumerate(far):
        out = far_blocks[i]
        if i >= 2 * quarter:
            out = after(out, own[far[i - 2 * quarter]])
        own[piece] = send(out, piece[0])
    for piece, out in zip(near, near_blocks):
        own[piece] = send(out, piece[0]) if piece[0] else out

    steps = [
        near[:1] + far[:quarter],
        far[quarter : 2 * quarter] + near[1:],
        far[2 * quarter : 3 * quarter],
        far[3 * quarter :],
    ]

    def score(pieces, partners, jobs, n_old, best, name, number, final=False):
        others = [part for piece in partners for part in sib[piece]]
        return pl.pallas_call(
            functools.partial(_score, pieces, jobs, len(partners), n_old, final),
            out_shape=jax.ShapeDtypeStruct((groups, slots), jnp.float32),
            in_specs=[SMEM] + [VMEM] * (1 + len(pieces) + len(others)),
            out_specs=VMEM,
            compiler_params=params,
            cost_estimate=pl.CostEstimate(flops=SCORE_COSTS[number], bytes_accessed=1, transcendentals=0),
            name=name,
        )(me, best, *[own[piece] for piece in pieces], *others)

    order, best, sib = [], jnp.zeros((groups, slots), jnp.float32), {}
    for number, step in enumerate(steps):
        for piece in step:
            ready = after(own[piece], best) if number >= HALVED else own[piece]
            cut = width // LANES // 2 * (piece[2] - piece[1])
            sib[piece] = [swap(part) for part in ((ready[:cut], ready[cut:]) if number == HALVED else (ready,))]
        n_old = len(order)
        order = order + step
        n = len(order)
        old, new = list(range(n_old)), list(range(n_old, n))
        if number < len(steps) - 1:
            jobs = [(new + [n + j for j in new], old)] if old else []
            best = score(order, order, jobs + [(list(range(2 * n)), new)], n_old, best, f"score_{number}", number)
        else:
            jobs = [(list(range(n + n_old)), new)]
            best = score(order, order[:n_old], jobs, n_old, best, f"score_{number}", number)
            jobs = [(new + list(range(n, 2 * n - n_old)), old + new)]
            best = score(order, step, jobs, n, best, "score_final", number, final=True)

    returned = lax.all_to_all(best, "wide", split_axis=0, concat_axis=0, tiled=True)
    return pl.pallas_call(
        functools.partial(_select, groups),
        out_shape=jax.ShapeDtypeStruct((rows,), jnp.float32),
        in_specs=[VMEM, VMEM, VMEM],
        out_specs=VMEM,
        compiler_params=params,
        name="select",
    )(lab, pos, returned)


def solution(mesh):
    in_specs = (
        P(("parts", "wide", "narrow"), None),
        P(("parts", "wide", "narrow"), None),
        P(("parts", "wide", "narrow")),
    )
    out_specs = P(("parts", "wide", "narrow"))
    return jax.shard_map(local, mesh=mesh, in_specs=in_specs, out_specs=out_specs, check_vma=False)
```

```python
import functools

import jax
import jax.numpy as jnp
from jax import lax
from jax.experimental import pallas as pl
from jax.experimental.pallas import tpu as pltpu
from jax.sharding import PartitionSpec as P

EMPTY = 2.0**22
VMEM_LIMIT = 40 * 1024 * 1024
LANES = 128
CHUNKS = 4
PACK_COST, SCORE_COSTS = 3 * 10**10, (10**10, 3 * 10**10, 1, 3 * 10**10)
HALVED = 2
TAIL = 16


def _nt(a, b):
    return lax.dot_general(a, b, (((1,), (1,)), ((), ())), preferred_element_type=jnp.float32)


def _as_bf16(mask):
    return mask.astype(jnp.float32).astype(jnp.bfloat16)


def _spans(slots):
    return -(-slots // LANES)


def _write_block(out, block, high, low, slots):
    scale = lax.rsqrt(jnp.sum(block * block, axis=1, keepdims=True) + 1e-06)
    block = (block * scale).astype(jnp.bfloat16)
    pieces = block.shape[1] // LANES
    for k in range(pieces):
        out[k * slots : (k + 1) * slots, :] = block[:, k * LANES : (k + 1) * LANES]
    spans = _spans(slots)
    lines = [part[:, i * LANES : (i + 1) * LANES] for part in (high, low) for i in range(spans)]
    lines.append(jnp.zeros((TAIL - 2 * spans, LANES), jnp.float32))
    out[pieces * slots :, :] = jnp.concatenate(lines, axis=0).astype(jnp.bfloat16)


def _block(parts, slots):
    pieces = [ref[k * slots : (k + 1) * slots, :] for ref in parts for k in range(ref.shape[0] // slots)]
    return jnp.concatenate(pieces, axis=1)


def _ranks(parts, slots):
    ref = parts[-1]
    tail = ref[ref.shape[0] - TAIL :, :].astype(jnp.float32)
    spans = _spans(slots)
    value = tail[:spans] * 256.0 + tail[spans : 2 * spans]
    return jnp.concatenate([value[i : i + 1] for i in range(spans)], axis=1)


def _pick(lab, pos, dest, low, high):
    key = jnp.where(lab == dest, pos, -1)
    return _as_bf16(lax.broadcasted_iota(jnp.int32, (high - low, lab.shape[1]), 0) + low == key)


def _pack_first(pieces, groups, slots, me_ref, emb_hbm, lab_hbm, prio_hbm, *rest):
    pos_ref, ranks_ref, *outs = rest[:-5]
    emb_ref, lab_ref, prio_ref, sems, word_sems = rest[-5:]
    rows = emb_ref.shape[0]
    words = [
        pltpu.make_async_copy(lab_hbm, lab_ref, word_sems.at[0]),
        pltpu.make_async_copy(prio_hbm, prio_ref, word_sems.at[1]),
    ]
    chunk = rows // CHUNKS
    spans = [pl.ds(i * chunk, chunk) for i in range(CHUNKS)]
    copies = [pltpu.make_async_copy(emb_hbm.at[span], emb_ref.at[span], sems.at[i]) for i, span in enumerate(spans)]
    for copy in words + copies:
        copy.start()
    earlier_rows = lax.broadcasted_iota(jnp.int32, (rows, rows), 0)
    before = _as_bf16(earlier_rows < lax.broadcasted_iota(jnp.int32, (rows, rows), 1))
    for copy in words:
        copy.wait()
    lab = lab_ref[...]
    away = jnp.bitwise_xor(lax.broadcasted_iota(jnp.int32, (groups, rows), 0), me_ref[0])
    onehot = (away == lab).astype(jnp.float32)
    earlier = jnp.dot(onehot.astype(jnp.bfloat16), before, preferred_element_type=jnp.float32)
    pos = jnp.sum(onehot * earlier, axis=0, keepdims=True).astype(jnp.int32)
    pos_ref[...] = pos
    prio = jnp.concatenate([prio_ref[i : i + 1, :] for i in range(rows // LANES)], axis=1)
    high = (prio >> 8).astype(jnp.float32)
    low = (prio & 255).astype(jnp.float32)
    parts = jnp.concatenate([onehot * high, onehot * low, onehot], axis=0).astype(jnp.bfloat16)
    places = lax.broadcasted_iota(jnp.int32, (_spans(slots) * LANES, rows), 0)
    placed = _nt(parts, _as_bf16(places == pos))
    high = jnp.where(placed[2 * groups :] > 0.5, placed[:groups], EMPTY)
    low = placed[groups : 2 * groups]
    ranks_ref[...] = jnp.concatenate([high, low], axis=0)
    picks = [_pick(lab, pos, jnp.bitwise_xor(me_ref[0], r), first, last) for r, first, last in pieces]
    for copy in copies:
        copy.wait()
    for (r, first, last), out, pick in zip(pieces, outs, picks):
        block = jnp.dot(pick, emb_ref[...], preferred_element_type=jnp.float32)
        _write_block(out, block, high[r : r + 1, first:], low[r : r + 1, first:], last - first)


def _pack_rest(pieces, groups, me_ref, emb_ref, lab_ref, pos_ref, ranks_ref, *outs):
    for (r, first, last), out in zip(pieces, outs):
        pick = _pick(lab_ref[...], pos_ref[...], jnp.bitwise_xor(me_ref[0], r), first, last)
        high = ranks_ref[r : r + 1, first:]
        low = ranks_ref[groups + r : groups + r + 1, first:]
        block = jnp.dot(pick, emb_ref[...], preferred_element_type=jnp.float32)
        _write_block(out, block, high, low, last - first)


def _score(pieces, jobs, n_sib, n_old, final, me_ref, prev_ref, *rest):
    n = len(pieces)
    out_ref, rest = rest[-1], list(rest[:-1])
    sib_pieces = pieces[n - n_sib :] if final else pieces[:n_sib]
    sizes = [last - first for _, first, last in list(pieces) + list(sib_pieces)]
    blocks = []
    while rest:
        parts = [rest.pop(0)]
        whole = parts[0].shape[0] % sizes[len(blocks)] == TAIL
        blocks.append(parts if whole else parts + [rest.pop(0)])
    ranks = [_ranks(parts, size) for parts, size in zip(blocks, sizes)]
    lanes = max(rank.shape[1] for rank in ranks)
    padded = [jnp.concatenate([rank] * (lanes // rank.shape[1]), axis=1) for rank in ranks]
    columns = jnp.transpose(jnp.concatenate(padded, axis=0))

    rows = [None] * n
    for j in range(n_old):
        r, first, last = pieces[j]
        rows[j] = prev_ref[r : r + 1, first:last]
    for keys, queries in jobs:
        sim = _nt(
            jnp.concatenate([_block(blocks[i], sizes[i]) for i in keys], axis=0),
            jnp.concatenate([_block(blocks[j], sizes[j]) for j in queries], axis=0),
        )
        key_ranks = jnp.concatenate([columns[: sizes[i], i : i + 1] for i in keys], axis=0)
        query_ranks = jnp.concatenate([ranks[j][:, : sizes[j]] for j in queries], axis=1)
        best = jnp.max(jnp.where(key_ranks < query_ranks, sim, -1.0), axis=0, keepdims=True)
        start = 0
        for j in queries:
            row = best[:, start : start + sizes[j]]
            rows[j] = row if rows[j] is None else jnp.maximum(rows[j], row)
            start += sizes[j]
    if not final:
        for (r, first, last), row in zip(pieces, rows):
            out_ref[r : r + 1, first:last] = row
    else:
        for r in range(out_ref.shape[0]):
            whole = [row for piece, row in sorted(zip(pieces, rows), key=lambda pair: pair[0]) if piece[0] == r]
            out_ref[pl.ds(jnp.bitwise_xor(me_ref[0], r), 1), :] = jnp.concatenate(whole, axis=1)


def _select(groups, lab_ref, pos_ref, got_ref, out_ref):
    slots = got_ref.shape[1]
    rows = lab_ref.shape[1]
    got = got_ref[...]
    a = got.astype(jnp.bfloat16)
    rest = got - a.astype(jnp.float32)
    b = rest.astype(jnp.bfloat16)
    c = (rest - b.astype(jnp.float32)).astype(jnp.bfloat16)
    pick = _as_bf16(lax.broadcasted_iota(jnp.int32, (slots, rows), 0) == pos_ref[...])
    value = jnp.dot(a, pick, preferred_element_type=jnp.float32)
    value += jnp.dot(b, pick, preferred_element_type=jnp.float32)
    value += jnp.dot(c, pick, preferred_element_type=jnp.float32)
    mine = lax.broadcasted_iota(jnp.int32, (groups, rows), 0) == lab_ref[...]
    out_ref[...] = jnp.sum(jnp.where(mine, value, 0.0), axis=0)


SMEM = pl.BlockSpec(memory_space=pltpu.SMEM)
VMEM = pl.BlockSpec(memory_space=pltpu.VMEM)
HBM = pl.BlockSpec(memory_space=pltpu.HBM)


def local(embeddings, labels, priority):
    rows, width = embeddings.shape
    groups = lax.axis_size("wide")
    slots = 2 * rows // groups
    half = groups // 2
    me = lax.axis_index("wide").astype(jnp.int32).reshape(1)
    lab = labels.reshape(1, rows)

    def block(piece):
        return jax.ShapeDtypeStruct((width // LANES * (piece[2] - piece[1]) + TAIL, LANES), jnp.bfloat16)

    quarter = max(1, half // 4)
    near = [(r, 0, slots) for r in range(half)]
    far = [(r, 0, slots) for r in range(half, groups)]
    params = pltpu.CompilerParams(vmem_limit_bytes=VMEM_LIMIT)

    def in_hbm(x):
        return pltpu.with_memory_space_constraint(x, pltpu.HBM)

    pos, ranks, *far_blocks = pl.pallas_call(
        functools.partial(_pack_first, far[:quarter], groups, slots),
        out_shape=[
            jax.ShapeDtypeStruct((1, rows), jnp.int32),
            jax.ShapeDtypeStruct((2 * groups, _spans(slots) * LANES), jnp.float32),
        ]
        + [block(piece) for piece in far[:quarter]],
        in_specs=[SMEM, HBM, HBM, HBM],
        out_specs=[VMEM] * (2 + quarter),
        scratch_shapes=[
            pltpu.VMEM((rows, width), jnp.bfloat16),
            pltpu.VMEM((1, rows), jnp.int32),
            pltpu.VMEM((rows // LANES, LANES), jnp.int32),
            pltpu.SemaphoreType.DMA((CHUNKS,)),
            pltpu.SemaphoreType.DMA((2,)),
        ],
        compiler_params=params,
        name="pack_first",
    )(me, in_hbm(embeddings), in_hbm(lab), in_hbm(priority.reshape(rows // LANES, LANES)))

    def swap(x):
        return lax.ppermute(x, "narrow", [(0, 1), (1, 0)])

    def send(x, r):
        return lax.ppermute(x, "wide", [(s, s ^ r) for s in range(groups)])

    def after(x, *others):
        return lax.optimization_barrier((x, *others))[0]

    def pack_rest(pieces, name):
        return pl.pallas_call(
            functools.partial(_pack_rest, pieces, groups),
            out_shape=[block(piece) for piece in pieces],
            in_specs=[SMEM] + [VMEM] * 4,
            out_specs=[VMEM] * len(pieces),
            compiler_params=params,
            cost_estimate=pl.CostEstimate(flops=PACK_COST, bytes_accessed=1, transcendentals=0),
            name=name,
        )(me, embeddings, lab, pos, ranks)

    later = pack_rest(far[quarter:] + near, "pack_rest")
    far_blocks += later[: -len(near)]
    near_blocks = later[-len(near) :]
    own = {}
    for i, piece in enumerate(far):
        out = far_blocks[i]
        if i >= 2 * quarter:
            out = after(out, own[far[i - 2 * quarter]])
        own[piece] = send(out, piece[0])
    for piece, out in zip(near, near_blocks):
        own[piece] = send(out, piece[0]) if piece[0] else out

    steps = [
        near[:1] + far[:quarter],
        far[quarter : 2 * quarter] + near[1:],
        far[2 * quarter : 3 * quarter],
        far[3 * quarter :],
    ]

    def score(pieces, partners, jobs, n_old, best, name, number, final=False):
        others = [part for piece in partners for part in sib[piece]]
        return pl.pallas_call(
            functools.partial(_score, pieces, jobs, len(partners), n_old, final),
            out_shape=jax.ShapeDtypeStruct((groups, slots), jnp.float32),
            in_specs=[SMEM] + [VMEM] * (1 + len(pieces) + len(others)),
            out_specs=VMEM,
            compiler_params=params,
            cost_estimate=pl.CostEstimate(flops=SCORE_COSTS[number], bytes_accessed=1, transcendentals=0),
            name=name,
        )(me, best, *[own[piece] for piece in pieces], *others)

    order, best, sib = [], jnp.zeros((groups, slots), jnp.float32), {}
    for number, step in enumerate(steps):
        for piece in step:
            ready = after(own[piece], best) if number >= HALVED else own[piece]
            cut = width // LANES // 2 * (piece[2] - piece[1])
            sib[piece] = [swap(part) for part in ((ready[:cut], ready[cut:]) if number == HALVED else (ready,))]
        n_old = len(order)
        order = order + step
        n = len(order)
        old, new = list(range(n_old)), list(range(n_old, n))
        if number < len(steps) - 1:
            jobs = [(new + [n + j for j in new], old)] if old else []
            best = score(order, order, jobs + [(list(range(2 * n)), new)], n_old, best, f"score_{number}", number)
        else:
            jobs = [(list(range(n + n_old)), new)]
            best = score(order, order[:n_old], jobs, n_old, best, f"score_{number}", number)
            jobs = [(new + list(range(n, 2 * n - n_old)), old + new)]
            best = score(order, step, jobs, n, best, "score_final", number, final=True)

    returned = lax.all_to_all(best, "wide", split_axis=0, concat_axis=0, tiled=True)
    return pl.pallas_call(
        functools.partial(_select, groups),
        out_shape=jax.ShapeDtypeStruct((rows,), jnp.float32),
        in_specs=[VMEM, VMEM, VMEM],
        out_specs=VMEM,
        compiler_params=params,
        name="select",
    )(lab, pos, returned)


def solution(mesh):
    in_specs = (
        P(("parts", "wide", "narrow"), None),
        P(("parts", "wide", "narrow"), None),
        P(("parts", "wide", "narrow")),
    )
    out_specs = P(("parts", "wide", "narrow"))
    return jax.shard_map(local, mesh=mesh, in_specs=in_specs, out_specs=out_specs, check_vma=False)
```
